32 devices in a mesh: row: 4 (over z), col: 8 (over y, x, core).
Axes of the slice: x: 2, y: 2, z: 4, core: 2. Of those that a mesh axis runs over, the one named last changes fastest.
Arguments:
- tokens: bfloat16 [128, 128, 512], P('row', 'col'), may hold values from -6 to 6
- norm_gains: float32 [4, 512], replicated, may hold values from 0.1 to 1.9
- qkv_weight: bfloat16 [2, 512, 1536], replicated, may hold values from -1 to 1
- rel_bias: float32 [2, 16, 13, 13], replicated, may hold values from -4 to 4
- proj_weight: bfloat16 [2, 512, 512], replicated, may hold values from -0.5 to 0.5
- up_weight: bfloat16 [2, 512, 2048], replicated, may hold values from -0.25 to 0.25
- down_weight: bfloat16 [2, 2048, 512], replicated, may hold values from -0.125 to 0.125
Outputs:
- features: bfloat16 [128, 128, 512], P('row', 'col')
The draws below stay inside these ranges and needn't reach their ends.
All inputs are finite; a program needn't handle non-finite values.
Results may differ from the reference program's by a relative error of at most 0.014.
Values may be sent and summed in bfloat16 or wider, within the bound.
A program may use at most 320 MiB of HBM per device.

```python
import math
import jax
import jax.numpy as jnp
from jax import lax

D = 512
HEADS = 16
FF = 2048
DILATION = 16
ROWS = 128
COLS = 128


def draw_qkv_weight(key, part):
    base_draw = jnp.clip(jax.random.normal(key, (2, D, 3 * D), jnp.float32), -4.0, 4.0) * D ** (-0.5)
    return jnp.clip(base_draw, -1.0, 1.0).astype(jnp.bfloat16)


def block_levels(rng, shape, split, low, top_value):
    level = 1.0
    for position, parts in split:
        heights = jax.random.uniform(jax.random.fold_in(jax.random.fold_in(rng, 6), position), (parts,), jnp.float32, low / len(split), top_value / len(split))
        level = level * jnp.repeat(jnp.exp(heights), shape[position] // parts).reshape((-1,) + (1,) * (len(shape) - 1 - position))
    return level


def noise(stream_key, dims, spread, bound, cuts=(), kind=jnp.bfloat16):
    gain = block_levels(stream_key, dims, cuts, -0.22, 0.18) if cuts else 1.0
    array = jax.random.normal(stream_key, dims, jnp.float32) * spread * gain
    return jnp.minimum(jnp.maximum(array, -bound), bound).astype(kind)


def setup_inputs(seed: int = 0) -> dict:
    splits = jax.random.split(jax.random.key(seed), 8)
    return {
        "tokens": noise(splits[0], (ROWS, COLS, D), 1.0, 6.0, ((0, 4), (1, 8))),
        "norm_gains": jnp.clip(1.0 + 0.18 * jax.random.normal(splits[1], (4, D), jnp.float32), 0.1, 1.9),
        "qkv_weight": draw_qkv_weight(jax.random.fold_in(splits[7], 71), 0),
        "rel_bias": noise(splits[3], (2, HEADS, 13, 13), 1.0, 4.0, (), jnp.float32),
        "proj_weight": noise(splits[4], (2, D, D), (D // 4) ** -0.5, 0.5),
        "up_weight": noise(splits[5], (2, D, FF), D ** -0.5, 0.25),
        "down_weight": noise(splits[6], (2, FF, D), FF ** -0.5, 0.125),
    }


def window_starts(positions, extent):
    return jnp.clip(positions - 3, 0, extent - 7)

def layer_norm(rows_in, norm_gain):
    values_f = rows_in.astype(jnp.float32)
    mean_value = lax.optimization_barrier(jnp.mean(values_f, axis=-1, keepdims=True))
    centred = values_f - mean_value
    variance = lax.optimization_barrier(jnp.mean(centred * centred, axis=-1, keepdims=True))
    return (centred * lax.rsqrt(variance + 1e-05) * norm_gain).astype(jnp.bfloat16)

def window_attend(queries, key_block, value_block, row_start, col_start, row_shift, col_shift, rel_table):
    query_rows, query_cols, group_count, feature_width = queries.shape
    head_count = rel_table.shape[0]
    head_size = feature_width // head_count
    split_query = queries.reshape(query_rows, query_cols, group_count, head_count, head_size).astype(jnp.float32)
    offsets = jnp.arange(7, dtype=jnp.int32)
    classes = jnp.arange(13, dtype=jnp.int32)
    col_index = col_start[None, :] + offsets[:, None]
    col_hot = ((col_shift[None, :] + offsets[:, None] + 6)[:, :, None] == classes).astype(jnp.float32)
    scaling = head_size ** (-0.5)
    score_list = []
    for offset in range(7):
        window = jnp.take(jnp.take(key_block, row_start + offset, axis=0), col_index, axis=1)
        window = window.reshape(query_rows, 7, query_cols, group_count, head_count, head_size).astype(jnp.float32)
        partial_score = jnp.einsum('icbnd,ixcbnd->ixcbn', split_query, window)
        row_hot = ((row_shift + offset + 6)[:, None] == classes).astype(jnp.float32)
        bias_term = jnp.einsum('iy,xcz,nyz->ixcn', row_hot, col_hot, rel_table, precision=lax.Precision.HIGHEST)
        score_list.append(partial_score * scaling + bias_term[:, :, :, None, :])
    scores = jnp.stack(score_list)
    row_max = lax.optimization_barrier(jnp.max(scores, axis=(0, 2), keepdims=True))
    exponent = jnp.exp(scores - row_max)
    weights = (exponent / lax.optimization_barrier(jnp.sum(exponent, axis=(0, 2), keepdims=True))).astype(jnp.bfloat16)
    running = jnp.zeros((query_rows, query_cols, group_count, head_count, head_size), jnp.float32)
    for offset in range(7):
        window = jnp.take(jnp.take(value_block, row_start + offset, axis=0), col_index, axis=1)
        window = window.reshape(query_rows, 7, query_cols, group_count, head_count, head_size).astype(jnp.float32)
        running = running + jnp.einsum('ixcbn,ixcbnd->icbnd', weights[offset].astype(jnp.float32), window)
    return running.reshape(query_rows, query_cols, group_count, feature_width).astype(jnp.bfloat16)

def row_blocks(function, arrays):
    count = arrays[0].shape[0]
    block = math.gcd(count, 4096)
    blocks = tuple((member.reshape(count // block, block, member.shape[1]) for member in arrays))
    result = lax.map(lambda pieces: function(*pieces), blocks)
    return result.reshape(count, result.shape[-1])

def project_inputs(rows_in, norm_gain, weight):
    return jnp.dot(layer_norm(rows_in, norm_gain), weight, preferred_element_type=jnp.float32).astype(jnp.bfloat16)

def finish_layer(attended, stream, norm_gain, proj, up_proj, down_proj):
    mixed = (jnp.dot(attended, proj, preferred_element_type=jnp.float32) + stream.astype(jnp.float32)).astype(jnp.bfloat16)
    normed = layer_norm(mixed, norm_gain)
    hidden = jax.nn.gelu(jnp.dot(normed, up_proj, preferred_element_type=jnp.float32), approximate=True).astype(jnp.bfloat16)
    return (jnp.dot(hidden, down_proj, preferred_element_type=jnp.float32) + mixed.astype(jnp.float32)).astype(jnp.bfloat16)

def reference(tokens, norm_gains, qkv_weight, rel_bias, proj_weight, up_weight, down_weight):
    map_rows, map_cols, feature_width = tokens.shape
    stream_rows = tokens.reshape(-1, feature_width)
    packed = row_blocks(lambda row_part: project_inputs(row_part, norm_gains[0], qkv_weight[0]), (stream_rows,))
    packed = packed.reshape(map_rows, map_cols, 1, 3 * feature_width)
    queries = packed[..., :feature_width]
    key_block = packed[..., feature_width:2 * feature_width]
    value_block = packed[..., 2 * feature_width:]
    row_begin = window_starts(jnp.arange(map_rows, dtype=jnp.int32), map_rows)
    col_places = jnp.arange(map_cols, dtype=jnp.int32)
    col_begin = window_starts(col_places, map_cols)

    def attend_block(block_index):
        first_row = block_index * 16
        part_query = lax.dynamic_slice_in_dim(queries, first_row, 16, 0)
        part_begin = lax.dynamic_slice_in_dim(row_begin, first_row, 16, 0)
        part_shift = part_begin - (first_row + jnp.arange(16, dtype=jnp.int32))
        return window_attend(part_query, key_block, value_block, part_begin, col_begin, part_shift, col_begin - col_places, rel_bias[0])
    attended = lax.map(attend_block, jnp.arange(map_rows // 16, dtype=jnp.int32)).reshape(-1, feature_width)
    stream_rows = row_blocks(lambda att_part, row_part: finish_layer(att_part, row_part, norm_gains[1], proj_weight[0], up_weight[0], down_weight[0]), (attended, stream_rows))
    group_rows = map_rows // DILATION
    group_cols = map_cols // DILATION
    grouped = stream_rows.reshape(group_rows, DILATION, group_cols, DILATION, feature_width).transpose(1, 3, 0, 2, 4)
    grouped_rows = grouped.reshape(-1, feature_width)
    packed_two = row_blocks(lambda row_part: project_inputs(row_part, norm_gains[2], qkv_weight[1]), (grouped_rows,))
    packed_two = packed_two.reshape(DILATION * DILATION // 16, 16, group_rows, group_cols, 3 * feature_width)
    grow_places = jnp.arange(group_rows, dtype=jnp.int32)
    gcol_places = jnp.arange(group_cols, dtype=jnp.int32)
    grow_begin = window_starts(grow_places, group_rows)
    gcol_begin = window_starts(gcol_places, group_cols)

    def attend_groups(group_part):
        placed = group_part.transpose(1, 2, 0, 3)
        result = window_attend(placed[..., :feature_width], placed[..., feature_width:2 * feature_width], placed[..., 2 * feature_width:], grow_begin, gcol_begin, grow_begin - grow_places, gcol_begin - gcol_places, rel_bias[1])
        return result.transpose(2, 0, 1, 3)
    attended_two = lax.map(attend_groups, packed_two).reshape(-1, feature_width)
    final_rows = row_blocks(lambda att_part, row_part: finish_layer(att_part, row_part, norm_gains[3], proj_weight[1], up_weight[1], down_weight[1]), (attended_two, grouped_rows))
    return final_rows.reshape(DILATION, DILATION, group_rows, group_cols, feature_width).transpose(2, 0, 3, 1, 4).reshape(map_rows, map_cols, feature_width)
```

```python
import functools
import math

import jax
import jax.numpy as jnp
from jax import lax
from jax.experimental import pallas as pl
from jax.experimental.pallas import tpu as pltpu
from jax.sharding import PartitionSpec as P

DILATION = 16
REACH = 6
HALO = 4
QUERY_ROWS = 8
MASKED = -1e30
LOG2E = 1.4426950408889634
VMEM_BYTES = 56 * 1024 * 1024


def layer_norm(values, gain):
    values_f = values.astype(jnp.float32)
    mean_value = jnp.mean(values_f, axis=-1, keepdims=True)
    centred = values_f - mean_value
    variance = jnp.mean(centred * centred, axis=-1, keepdims=True)
    return (centred * lax.rsqrt(variance + 1e-05) * gain).astype(jnp.bfloat16)


def dot(left, right):
    return jnp.dot(left, right, preferred_element_type=jnp.float32)


def bias_rows(rel, q_rows, k_rows, q_cols, k_cols, row_off, col_off):
    heads, classes, _ = rel.shape
    extent = q_rows + k_rows - 1
    before = q_rows - 1 + row_off - REACH
    left = q_cols + col_off
    padded = jnp.pad(
        rel * LOG2E,
        ((0, 0), (before, extent - before - classes), (left, k_cols + q_cols)),
    )
    starts = [left + REACH - col_off - place for place in range(q_cols)]
    rows = [padded[:, :, start : start + k_cols] for start in starts]
    return jnp.stack(rows, axis=1).reshape(heads, q_cols, extent * k_cols)


def in_window(query, key, extent):
    start = jnp.clip(query - 3, 0, extent - 7)
    return (key >= start) & (key < start + 7)


def head_lanes(lanes, head_size):
    lane = lax.broadcasted_iota(jnp.int32, (1, lanes), 1)
    return [(lane // head_size) == h for h in range(lanes // head_size)]


def attend(queries, keys, values, bias, mask, head_size):
    count, lanes = queries.shape
    picks = head_lanes(lanes, head_size)
    zero = jnp.zeros_like(queries)
    stacked = jnp.concatenate([jnp.where(pick, queries, zero) for pick in picks], axis=0)
    scores = lax.dot_general(
        stacked, keys, (((1,), (1,)), ((), ())), preferred_element_type=jnp.float32
    )
    scores = scores.reshape(len(picks), count, keys.shape[0]) + bias
    if mask is not None:
        scores = scores + mask[None]
    peak = jnp.max(scores, axis=-1, keepdims=True)
    weights = jnp.exp2(scores - peak).astype(jnp.bfloat16)
    wide = jnp.concatenate([values, jnp.ones_like(values)], axis=1)
    summed = dot(weights.reshape(len(picks) * count, keys.shape[0]), wide)
    ratio = summed[:, :lanes] / summed[:, lanes:]
    result = ratio[:count]
    for h in range(1, len(picks)):
        result = jnp.where(picks[h], ratio[h * count : (h + 1) * count], result)
    return result.astype(jnp.bfloat16)


def finish(att_ref, x_ref, gain, proj_ref, up_ref, down_ref, out_ref, chunk):
    width = x_ref.shape[1]
    hidden_width = up_ref.shape[1]
    part = math.gcd(hidden_width, 512)

    def step(index, carry):
        rows = pl.ds(pl.multiple_of(index * chunk, chunk), chunk)
        mixed = (dot(att_ref[rows, :], proj_ref[...]) + x_ref[rows, :].astype(jnp.float32)).astype(
            jnp.bfloat16
        )
        normed = layer_norm(mixed, gain)
        total = mixed.astype(jnp.float32)
        for first in range(0, hidden_width, part):
            hidden = jax.nn.gelu(dot(normed, up_ref[:, first : first + part]), approximate=True)
            total = total + dot(hidden.astype(jnp.bfloat16), down_ref[first : first + part, :])
        out_ref[rows, :] = total.astype(jnp.bfloat16)
        return carry

    lax.fori_loop(0, x_ref.shape[0] // chunk, step, 0)


def project(src_ref, gain, weight, dst_ref, scale, chunk):
    def step(index, carry):
        rows = pl.ds(pl.multiple_of(index * chunk, chunk), chunk)
        result = dot(layer_norm(src_ref[rows, :], gain), weight)
        if scale is not None:
            result = result * scale
        dst_ref[rows, :] = result.astype(jnp.bfloat16)
        return carry

    lax.fori_loop(0, src_ref.shape[0] // chunk, step, 0)


def local_kernel(
    geometry, x_ref, pad_ref, gains_ref, qkv_ref, bias_ref, proj_ref, up_ref, down_ref, out_ref,
    q_ref, kv_ref, full_ref, att_ref,
):
    tile_rows, tile_cols, map_rows, map_cols, heads = geometry
    width = x_ref.shape[1]
    head_size = width // heads
    lanes = 128
    per = lanes // head_size
    wide_cols = tile_cols + 2 * HALO
    key_rows = QUERY_ROWS + 2 * HALO
    n_query = QUERY_ROWS * tile_cols
    n_key = key_rows * wide_cols
    scale = head_size ** (-0.5) * LOG2E
    gain = gains_ref[0:1, :]
    for n in range(heads):
        for i in range(QUERY_ROWS):
            start = (QUERY_ROWS - 1 - i) * wide_cols
            full_ref[n, i * tile_cols : (i + 1) * tile_cols, :] = bias_ref[n, :, start : start + n_key]
    project(x_ref, gain, qkv_ref[:, :width], q_ref, scale, 256)
    project(pad_ref, gain, qkv_ref[:, width:], kv_ref, None, math.gcd(pad_ref.shape[0], 320))
    first_row = lax.axis_index("row") * tile_rows
    first_col = lax.axis_index("col") * tile_cols
    query = lax.broadcasted_iota(jnp.int32, (n_query, 1), 0)
    key = lax.broadcasted_iota(jnp.int32, (1, n_key), 1)
    query_row = query // tile_cols
    query_col = first_col + query - query_row * tile_cols
    key_row = key // wide_cols
    key_col = first_col + key - key_row * wide_cols - HALO
    col_seen = in_window(query_col, key_col, map_cols)

    def step(block, carry):
        top = first_row + block * QUERY_ROWS
        seen = col_seen & in_window(top + query_row, top + key_row - HALO, map_rows)
        mask = jnp.where(seen, 0.0, MASKED).astype(jnp.float32)
        q_rows = pl.ds(pl.multiple_of(block * n_query, n_query), n_query)
        k_first = QUERY_ROWS * wide_cols
        k_rows = pl.ds(pl.multiple_of(block * k_first, k_first), n_key)
        for g in range(width // lanes):
            cols = slice(g * lanes, (g + 1) * lanes)
            v_cols = slice(width + g * lanes, width + (g + 1) * lanes)
            att_ref[q_rows, cols] = attend(
                q_ref[q_rows, cols],
                kv_ref[k_rows, cols],
                kv_ref[k_rows, v_cols],
                full_ref[g * per : (g + 1) * per],
                mask,
                head_size,
            )
        return carry

    lax.fori_loop(0, tile_rows // QUERY_ROWS, step, 0)
    finish(att_ref, x_ref, gains_ref[1:2, :], proj_ref, up_ref, down_ref, out_ref, 256)


def group_kernel(
    geometry, x_ref, gains_ref, qkv_ref, bias_ref, proj_ref, up_ref, down_ref, out_ref,
    q_ref, kv_ref, full_ref, att_ref,
):
    group_rows, group_cols, heads, pack = geometry
    width = x_ref.shape[1]
    head_size = width // heads
    lanes = 128
    per = lanes // head_size
    size = group_rows * group_cols
    n_query = pack * size
    scale = head_size ** (-0.5) * LOG2E
    gain = gains_ref[2:3, :]
    query = lax.broadcasted_iota(jnp.int32, (n_query, 1), 0)
    key = lax.broadcasted_iota(jnp.int32, (1, n_query), 1)
    query_row, key_row = query // group_cols, key // group_cols
    query_col, key_col = query - query_row * group_cols, key - key_row * group_cols
    query_group, key_group = query // size, key // size
    seen = (
        (query_group == key_group)
        & in_window(query_row - query_group * group_rows, key_row - key_group * group_rows, group_rows)
        & in_window(query_col, key_col, group_cols)
    )
    for n in range(heads):
        for i in range(group_rows):
            start = (group_rows - 1 - i) * group_cols
            strip = bias_ref[n, :, start : start + size]
            strip = jnp.concatenate([strip] * pack, axis=1)
            for t in range(pack):
                first = t * size + i * group_cols
                full_ref[n, first : first + group_cols, :] = strip
        full_ref[n] = jnp.where(seen, full_ref[n], MASKED)
    project(x_ref, gain, qkv_ref[:, :width], q_ref, scale, 256)
    project(x_ref, gain, qkv_ref[:, width:], kv_ref, None, 256)

    def step(block, carry):
        rows = pl.ds(pl.multiple_of(block * n_query, n_query), n_query)
        for g in range(width // lanes):
            cols = slice(g * lanes, (g + 1) * lanes)
            v_cols = slice(width + g * lanes, width + (g + 1) * lanes)
            att_ref[rows, cols] = attend(
                q_ref[rows, cols],
                kv_ref[rows, cols],
                kv_ref[rows, v_cols],
                full_ref[g * per : (g + 1) * per],
                None,
                head_size,
            )
        return carry

    lax.fori_loop(0, x_ref.shape[0] // n_query, step, 0)
    finish(att_ref, x_ref, gains_ref[3:4, :], proj_ref, up_ref, down_ref, out_ref, 256)


def whole(array):
    return pl.BlockSpec(array.shape, lambda i: (0,) * array.ndim)


def one_layer(array, layer):
    return pl.BlockSpec((None,) + array.shape[1:], lambda i: (layer,) + (0,) * (array.ndim - 1))


def call_layer(kernel, layer, acts, gains, bias, weights, key_count, n_query, n_key):
    qkv, proj, up, down = weights
    rows, width = acts[0].shape
    heads = bias.shape[0]
    return pl.pallas_call(
        kernel,
        grid=(1,),
        out_shape=jax.ShapeDtypeStruct((rows, width), jnp.bfloat16),
        in_specs=[whole(act) for act in acts]
        + [whole(gains), one_layer(qkv, layer), whole(bias)]
        + [one_layer(weight, layer) for weight in (proj, up, down)],
        out_specs=pl.BlockSpec((rows, width), lambda i: (0, 0)),
        scratch_shapes=[
            pltpu.VMEM((rows, width), jnp.bfloat16),
            pltpu.VMEM((key_count, 2 * width), jnp.bfloat16),
            pltpu.VMEM((heads, n_query, n_key), jnp.float32),
            pltpu.VMEM((rows, width), jnp.bfloat16),
        ],
        compiler_params=pltpu.CompilerParams(vmem_limit_bytes=VMEM_BYTES),
    )(*acts, gains, qkv, bias, proj, up, down)


def padded(cells, axis, dim, width):
    count = lax.axis_size(axis)
    head = lax.slice_in_dim(cells, 0, width, axis=dim)
    tail = lax.slice_in_dim(cells, cells.shape[dim] - width, cells.shape[dim], axis=dim)
    return jnp.concatenate(
        [
            lax.ppermute(tail, axis, [(i, i + 1) for i in range(count - 1)]),
            cells,
            lax.ppermute(head, axis, [(i + 1, i) for i in range(count - 1)]),
        ],
        axis=dim,
    )


def body(tokens, norm_gains, qkv_weight, rel_bias, proj_weight, up_weight, down_weight):
    tile_rows, tile_cols, width = tokens.shape
    row_count = lax.axis_size("row")
    col_count = lax.axis_size("col")
    map_rows = tile_rows * row_count
    map_cols = tile_cols * col_count
    heads = rel_bias.shape[1]
    weights = (qkv_weight, proj_weight, up_weight, down_weight)
    residue_rows = DILATION // row_count
    residue_cols = DILATION // col_count
    block_rows = tile_rows // DILATION
    block_cols = tile_cols // DILATION
    group_rows = block_rows * row_count
    group_cols = block_cols * col_count
    size = group_rows * group_cols

    key_rows = QUERY_ROWS + 2 * HALO
    wide_cols = tile_cols + 2 * HALO
    bias_one = bias_rows(rel_bias[0], QUERY_ROWS, key_rows, tile_cols, wide_cols, HALO, HALO)
    bias_two = bias_rows(rel_bias[1], group_rows, group_rows, group_cols, group_cols, 0, 0)

    rim = padded(padded(tokens, "row", 0, HALO), "col", 1, HALO).reshape(-1, width)
    stream = call_layer(
        functools.partial(local_kernel, (tile_rows, tile_cols, map_rows, map_cols, heads)),
        0,
        (tokens.reshape(-1, width), rim),
        norm_gains,
        bias_one,
        weights,
        rim.shape[0],
        QUERY_ROWS * tile_cols,
        key_rows * wide_cols,
    )
    shaped = stream.reshape(
        block_rows, row_count, residue_rows, block_cols, col_count, residue_cols, width
    )
    shaped = shaped.transpose(1, 4, 2, 5, 0, 3, 6).reshape(
        row_count * col_count, residue_rows, residue_cols, block_rows * block_cols, width
    )
    arrived = lax.all_to_all(shaped, ("row", "col"), split_axis=0, concat_axis=0, tiled=True)
    grouped = arrived.reshape(
        row_count, col_count, residue_rows, residue_cols, block_rows, block_cols, width
    )
    grouped = grouped.transpose(2, 3, 0, 4, 1, 5, 6).reshape(-1, width)
    pack = max(1, 128 // size)
    final = call_layer(
        functools.partial(group_kernel, (group_rows, group_cols, heads, pack)),
        1,
        (grouped,),
        norm_gains,
        bias_two,
        weights,
        grouped.shape[0],
        pack * size,
        pack * size,
    )
    shaped = final.reshape(
        residue_rows, residue_cols, row_count, block_rows, col_count, block_cols, width
    )
    shaped = shaped.transpose(2, 4, 0, 1, 3, 5, 6).reshape(
        row_count * col_count, residue_rows, residue_cols, block_rows * block_cols, width
    )
    arrived = lax.all_to_all(shaped, ("row", "col"), split_axis=0, concat_axis=0, tiled=True)
    restored = arrived.reshape(
        row_count, col_count, residue_rows, residue_cols, block_rows, block_cols, width
    )
    return restored.transpose(4, 0, 2, 5, 1, 3, 6).reshape(tile_rows, tile_cols, width)


def solution(mesh):
    placed = (P("row", "col", None), P(), P(), P(), P(), P(), P())
    return jax.shard_map(
        body, mesh=mesh, in_specs=placed, out_specs=P("row", "col", None), check_vma=False
    )
```

```python
import functools
import math

import jax
import jax.numpy as jnp
from jax import lax
from jax.experimental import pallas as pl
from jax.experimental.pallas import tpu as pltpu
from jax.sharding import PartitionSpec as P

DILATION = 16
REACH = 6
HALO = 4
QUERY_ROWS = 8
MASKED = -1e30
LOG2E = 1.4426950408889634
VMEM_BYTES = 56 * 1024 * 1024


def layer_norm(values, gain):
    values_f = values.astype(jnp.float32)
    mean_value = jnp.mean(values_f, axis=-1, keepdims=True)
    centred = values_f - mean_value
    variance = jnp.mean(centred * centred, axis=-1, keepdims=True)
    return (centred * lax.rsqrt(variance + 1e-05) * gain).astype(jnp.bfloat16)


def dot(left, right):
    return jnp.dot(left, right, preferred_element_type=jnp.float32)


def fill_bias(rel_ref, rows_ref, full_ref, q_rows, k_rows, row_off, k_cols, col_places, first_key, groups):
    heads, entries = rel_ref.shape
    classes = math.isqrt(entries)
    q_cols = rows_ref.shape[1] // heads
    extent = q_rows + k_rows - 1
    before = q_rows - 1 + row_off - REACH
    chunks = -(-extent * k_cols // 128)
    width = chunks * 128
    place = lax.broadcasted_iota(jnp.int32, (1, width), 1)
    entry = lax.broadcasted_iota(jnp.int32, (entries, 1), 0)
    across = place // k_cols
    key_col = col_places(place - across * k_cols)
    down = across - before
    table = rel_ref[...] * LOG2E
    for j in range(q_cols):
        over = key_col - j + REACH
        known = (down >= 0) & (down < classes) & (over >= 0) & (over < classes)
        target = jnp.where(known, down * classes + over, -1)
        hot = (entry == target).astype(jnp.float32)
        found = jnp.dot(
            table, hot, precision=lax.Precision.HIGHEST, preferred_element_type=jnp.float32
        )
        for c in range(chunks):
            rows_ref[c, j * heads : (j + 1) * heads, :] = found[:, c * 128 : (c + 1) * 128]
    n_key = k_rows * k_cols
    for n in range(heads):
        strips = jnp.concatenate(
            [rows_ref[c, pl.ds(n, q_cols, stride=heads), :] for c in range(chunks)], axis=1
        )
        for i in range(q_rows):
            start = (q_rows - 1 - i) * k_cols
            strip = jnp.concatenate([strips[:, start : start + n_key]] * groups, axis=1)
            for t in range(groups):
                first = t * n_key + i * q_cols
                full_ref[n, first : first + q_cols, first_key : first_key + groups * n_key] = strip


def slot_places(index, shape):
    tile_cols, residue_rows, residue_cols, block_rows, block_cols, col_count, slot = shape
    row = index // tile_cols
    col = index - row * tile_cols
    row_block = row // DILATION
    col_block = col // DILATION
    row, col = row - row_block * DILATION, col - col_block * DILATION
    peer_row = row // residue_rows
    peer_col = col // residue_cols
    inner = (row - peer_row * residue_rows) * residue_cols + col - peer_col * residue_cols
    inner = (inner * block_rows + row_block) * block_cols + col_block
    return (peer_row * col_count + peer_col) * slot + inner


def group_places(index, shape):
    _, residue_rows, residue_cols, block_rows, block_cols, col_count, slot, row_count = shape
    used = residue_rows * residue_cols * block_rows * block_cols
    peer = index // slot
    inner = index - peer * slot
    peer_row = peer // col_count
    peer_col = peer - peer_row * col_count
    rest = inner // block_cols
    col_block = inner - rest * block_cols
    residue = rest // block_rows
    row_block = rest - residue * block_rows
    place = residue * (block_rows * row_count) + peer_row * block_rows + row_block
    place = place * (block_cols * col_count) + peer_col * block_cols + col_block
    return jnp.where(inner < used, place, -1)


def column(count):
    return lax.broadcasted_iota(jnp.int32, (count, 1), 0)


def line(count):
    return lax.broadcasted_iota(jnp.int32, (1, count), 1)


def one_hot(left, right):
    return jnp.where(left == right, 1.0, 0.0).astype(jnp.bfloat16)


def in_window(query, key, extent):
    start = jnp.clip(query - 3, 0, extent - 7)
    return (key >= start) & (key < start + 7)


def head_lanes(lanes, head_size):
    lane = lax.broadcasted_iota(jnp.int32, (1, lanes), 1)
    return [(lane // head_size) == h for h in range(lanes // head_size)]


def attend(queries, keys, values, bias, mask, head_size):
    count, lanes = queries.shape
    picks = head_lanes(lanes, head_size)
    zero = jnp.zeros_like(queries)
    stacked = jnp.concatenate([jnp.where(pick, queries, zero) for pick in picks], axis=0)
    scores = lax.dot_general(
        stacked, keys, (((1,), (1,)), ((), ())), preferred_element_type=jnp.float32
    )
    scores = scores.reshape(len(picks), count, keys.shape[0]) + bias
    if mask is not None:
        scores = scores + mask[None]
    peak = jnp.max(scores, axis=-1, keepdims=True)
    weights = jnp.exp2(scores - peak).astype(jnp.bfloat16)
    wide = jnp.concatenate([values, jnp.ones_like(values)], axis=1)
    summed = dot(weights.reshape(len(picks) * count, keys.shape[0]), wide)
    ratio = summed[:, :lanes] / summed[:, lanes:]
    result = ratio[:count]
    for h in range(1, len(picks)):
        result = jnp.where(picks[h], ratio[h * count : (h + 1) * count], result)
    return result.astype(jnp.bfloat16)


def finish(att_ref, x_ref, gain, proj_ref, up_ref, down_ref, out_ref, chunk):
    width = x_ref.shape[1]
    hidden_width = up_ref.shape[1]
    part = math.gcd(hidden_width, 512)

    def step(index, carry):
        rows = pl.ds(pl.multiple_of(index * chunk, chunk), chunk)
        mixed = (dot(att_ref[rows, :], proj_ref[...]) + x_ref[rows, :].astype(jnp.float32)).astype(
            jnp.bfloat16
        )
        normed = layer_norm(mixed, gain)
        total = mixed.astype(jnp.float32)
        for first in range(0, hidden_width, part):
            hidden = jax.nn.gelu(dot(normed, up_ref[:, first : first + part]), approximate=True)
            total = total + dot(hidden.astype(jnp.bfloat16), down_ref[first : first + part, :])
        out_ref[rows, :] = total.astype(jnp.bfloat16)
        return carry

    lax.fori_loop(0, x_ref.shape[0] // chunk, step, 0)


def project(src_ref, gain, weight, dst_ref, scale, chunk):
    def step(index, carry):
        rows = pl.ds(pl.multiple_of(index * chunk, chunk), chunk)
        result = dot(layer_norm(src_ref[rows, :], gain), weight)
        if scale is not None:
            result = result * scale
        dst_ref[rows, :] = result.astype(jnp.bfloat16)
        return carry

    lax.fori_loop(0, src_ref.shape[0] // chunk, step, 0)


def local_kernel(
    geometry, x_ref, above_ref, below_ref, left_ref, right_ref, gains_ref, qkv_ref, rel_ref,
    proj_ref, up_ref, down_ref, out_ref, q_ref, kv_ref, full_ref, att_ref, bias_ref, pad_ref,
):
    tile_rows, tile_cols, map_rows, map_cols, heads, places = geometry
    tokens, width = x_ref.shape
    head_size = width // heads
    lanes = 128
    per = lanes // head_size
    key_rows = QUERY_ROWS + 2 * HALO
    n_query = QUERY_ROWS * tile_cols
    scale = head_size ** (-0.5) * LOG2E
    gain = gains_ref[0:1, :]
    rim = HALO * tile_cols
    side = (tile_rows + 2 * HALO) * HALO
    own = tokens + 2 * rim
    pad_ref[0:rim, :] = above_ref[...]
    pad_ref[rim : rim + tokens, :] = x_ref[...]
    pad_ref[rim + tokens : own, :] = below_ref[...]
    pad_ref[own : own + side, :] = left_ref[...]
    pad_ref[own + side :, :] = right_ref[...]
    sets = (
        (0, tile_cols, 0, lambda col: col),
        (own, HALO, key_rows * tile_cols, lambda col: col - HALO),
        (own + side, HALO, key_rows * (tile_cols + HALO), lambda col: col + tile_cols),
    )
    for _, k_cols, first_key, col_places in sets:
        fill_bias(
            rel_ref, bias_ref, full_ref, QUERY_ROWS, key_rows, HALO, k_cols, col_places, first_key, 1
        )
    project(x_ref, gain, qkv_ref[:, :width], q_ref, scale, 256)
    project(pad_ref, gain, qkv_ref[:, width:], kv_ref, None, math.gcd(pad_ref.shape[0], 320))
    first_row = lax.axis_index("row") * tile_rows
    first_col = lax.axis_index("col") * tile_cols
    query = column(n_query)
    query_row = query // tile_cols
    query_col = first_col + query - query_row * tile_cols
    seen_cols, key_row_list = [], []
    for _, k_cols, _, col_places in sets:
        key = line(key_rows * k_cols)
        key_row = key // k_cols
        key_row_list.append(key_row)
        key_col = first_col + col_places(key - key_row * k_cols)
        seen_cols.append(in_window(query_col, key_col, map_cols))

    def step(block, carry):
        top = first_row + block * QUERY_ROWS
        masks = [
            jnp.where(col_seen & in_window(top + query_row, top + key_row - HALO, map_rows), 0.0, MASKED)
            for col_seen, key_row in zip(seen_cols, key_row_list)
        ]
        mask = jnp.concatenate(masks, axis=1).astype(jnp.float32)
        q_rows = pl.ds(pl.multiple_of(block * n_query, n_query), n_query)
        k_rows = []
        for base, k_cols, _, _ in sets:
            stride = QUERY_ROWS * k_cols
            k_rows.append(pl.ds(pl.multiple_of(base + block * stride, 16), key_rows * k_cols))
        for g in range(width // lanes):
            cols = slice(g * lanes, (g + 1) * lanes)
            v_cols = slice(width + g * lanes, width + (g + 1) * lanes)
            att_ref[q_rows, cols] = attend(
                q_ref[q_rows, cols],
                jnp.concatenate([kv_ref[rows, cols] for rows in k_rows], axis=0),
                jnp.concatenate([kv_ref[rows, v_cols] for rows in k_rows], axis=0),
                full_ref[g * per : (g + 1) * per],
                mask,
                head_size,
            )
        return carry

    lax.fori_loop(0, tile_rows // QUERY_ROWS, step, 0)
    finish(att_ref, x_ref, gains_ref[1:2, :], proj_ref, up_ref, down_ref, q_ref, 256)
    hot = one_hot(column(out_ref.shape[0]), slot_places(line(tokens), places[:7]))
    out_ref[...] = dot(hot, q_ref[...]).astype(jnp.bfloat16)


def group_kernel(
    geometry, in_ref, gains_ref, qkv_ref, rel_ref, proj_ref, up_ref, down_ref, out_ref,
    q_ref, kv_ref, full_ref, att_ref, bias_ref, x_ref,
):
    group_rows, group_cols, heads, pack, places = geometry
    tokens, width = x_ref.shape
    arrivals = in_ref.shape[0]
    head_size = width // heads
    lanes = 128
    per = lanes // head_size
    size = group_rows * group_cols
    n_query = pack * size
    scale = head_size ** (-0.5) * LOG2E
    gain = gains_ref[2:3, :]
    hot = one_hot(column(tokens), group_places(line(arrivals), places))
    x_ref[...] = dot(hot, in_ref[...]).astype(jnp.bfloat16)
    query = column(n_query)
    key = line(n_query)
    query_row, key_row = query // group_cols, key // group_cols
    query_col, key_col = query - query_row * group_cols, key - key_row * group_cols
    query_group, key_group = query // size, key // size
    seen = (
        (query_group == key_group)
        & in_window(query_row - query_group * group_rows, key_row - key_group * group_rows, group_rows)
        & in_window(query_col, key_col, group_cols)
    )
    fill_bias(
        rel_ref, bias_ref, full_ref, group_rows, group_rows, 0, group_cols, lambda col: col, 0, pack
    )
    for n in range(heads):
        full_ref[n] = jnp.where(seen, full_ref[n], MASKED)
    project(x_ref, gain, qkv_ref[:, :width], q_ref, scale, 256)
    project(x_ref, gain, qkv_ref[:, width:], kv_ref, None, 256)

    def step(block, carry):
        rows = pl.ds(pl.multiple_of(block * n_query, n_query), n_query)
        for g in range(width // lanes):
            cols = slice(g * lanes, (g + 1) * lanes)
            v_cols = slice(width + g * lanes, width + (g + 1) * lanes)
            att_ref[rows, cols] = attend(
                q_ref[rows, cols],
                kv_ref[rows, cols],
                kv_ref[rows, v_cols],
                full_ref[g * per : (g + 1) * per],
                None,
                head_size,
            )
        return carry

    lax.fori_loop(0, tokens // n_query, step, 0)
    finish(att_ref, x_ref, gains_ref[3:4, :], proj_ref, up_ref, down_ref, q_ref, 256)
    back = one_hot(group_places(column(arrivals), places), line(tokens))
    out_ref[...] = dot(back, q_ref[...]).astype(jnp.bfloat16)


def place_kernel(places, in_ref, out_ref):
    hot = one_hot(slot_places(column(out_ref.shape[0]), places[:7]), line(in_ref.shape[0]))
    out_ref[...] = dot(hot, in_ref[...]).astype(jnp.bfloat16)


def whole(array):
    return pl.BlockSpec(array.shape, lambda i: (0,) * array.ndim)


def one_layer(array, layer):
    return pl.BlockSpec((None,) + array.shape[1:], lambda i: (layer,) + (0,) * (array.ndim - 1))


def call_layer(kernel, layer, acts, gains, rel, weights, out_rows, tokens, key_count, n_query, n_key, bias, pad):
    qkv, proj, up, down = weights
    width = acts[0].shape[1]
    heads = rel.shape[1]
    q_cols, bias_width = bias
    return pl.pallas_call(
        kernel,
        grid=(1,),
        out_shape=jax.ShapeDtypeStruct((out_rows, width), jnp.bfloat16),
        in_specs=[whole(act) for act in acts]
        + [whole(gains), one_layer(qkv, layer), one_layer(rel, layer)]
        + [one_layer(weight, layer) for weight in (proj, up, down)],
        out_specs=pl.BlockSpec((out_rows, width), lambda i: (0, 0)),
        scratch_shapes=[
            pltpu.VMEM((tokens, width), jnp.bfloat16),
            pltpu.VMEM((key_count, 2 * width), jnp.bfloat16),
            pltpu.VMEM((heads, n_query, n_key), jnp.float32),
            pltpu.VMEM((tokens, width), jnp.bfloat16),
            pltpu.VMEM((-(-bias_width // 128), q_cols * heads, 128), jnp.float32),
            pltpu.VMEM((pad, width), jnp.bfloat16),
        ],
        compiler_params=pltpu.CompilerParams(vmem_limit_bytes=VMEM_BYTES),
    )(*acts, gains, qkv, rel, proj, up, down)


def from_both(cells, axis, dim, width):
    count = lax.axis_size(axis)
    head = lax.slice_in_dim(cells, 0, width, axis=dim)
    tail = lax.slice_in_dim(cells, cells.shape[dim] - width, cells.shape[dim], axis=dim)
    return (
        lax.ppermute(tail, axis, [(i, i + 1) for i in range(count - 1)]),
        lax.ppermute(head, axis, [(i + 1, i) for i in range(count - 1)]),
    )


def body(tokens, norm_gains, qkv_weight, rel_bias, proj_weight, up_weight, down_weight):
    tile_rows, tile_cols, width = tokens.shape
    row_count = lax.axis_size("row")
    col_count = lax.axis_size("col")
    heads = rel_bias.shape[1]
    rel = rel_bias.reshape(rel_bias.shape[0], heads, -1)
    weights = (qkv_weight, proj_weight, up_weight, down_weight)
    residue_rows = DILATION // row_count
    residue_cols = DILATION // col_count
    block_rows = tile_rows // DILATION
    block_cols = tile_cols // DILATION
    group_rows = block_rows * row_count
    group_cols = block_cols * col_count
    size = group_rows * group_cols
    peers = row_count * col_count
    count = tile_rows * tile_cols
    slot = -(-(count // peers) // 16) * 16
    places = (
        tile_cols, residue_rows, residue_cols, block_rows, block_cols, col_count, slot, row_count
    )

    key_rows = QUERY_ROWS + 2 * HALO
    above, below = from_both(tokens, "row", 0, HALO)
    edges = jnp.concatenate(
        [
            jnp.concatenate([above[:, :HALO], tokens[:, :HALO], below[:, :HALO]], axis=0),
            jnp.concatenate([above[:, -HALO:], tokens[:, -HALO:], below[:, -HALO:]], axis=0),
        ],
        axis=1,
    )
    left, right = from_both(edges, "col", 1, HALO)
    flat = [piece.reshape(-1, width) for piece in (tokens, above, below, left, right)]
    pad = sum(piece.shape[0] for piece in flat)
    wide_cols = tile_cols + 2 * HALO
    sent = call_layer(
        functools.partial(
            local_kernel,
            (tile_rows, tile_cols, tile_rows * row_count, tile_cols * col_count, heads, places),
        ),
        0,
        flat,
        norm_gains,
        rel,
        weights,
        peers * slot,
        count,
        pad,
        QUERY_ROWS * tile_cols,
        key_rows * wide_cols,
        (tile_cols, (QUERY_ROWS + key_rows - 1) * tile_cols),
        pad,
    )
    arrived = lax.all_to_all(
        sent.reshape(peers, slot, width), ("row", "col"), split_axis=0, concat_axis=0, tiled=True
    ).reshape(-1, width)
    pack = max(1, 128 // size)
    sent = call_layer(
        functools.partial(group_kernel, (group_rows, group_cols, heads, pack, places)),
        1,
        [arrived],
        norm_gains,
        rel,
        weights,
        peers * slot,
        count,
        count,
        pack * size,
        pack * size,
        (group_cols, (2 * group_rows - 1) * group_cols),
        count,
    )
    arrived = lax.all_to_all(
        sent.reshape(peers, slot, width), ("row", "col"), split_axis=0, concat_axis=0, tiled=True
    ).reshape(-1, width)
    placed = pl.pallas_call(
        functools.partial(place_kernel, places),
        out_shape=jax.ShapeDtypeStruct((count, width), jnp.bfloat16),
        compiler_params=pltpu.CompilerParams(vmem_limit_bytes=VMEM_BYTES),
    )(arrived)
    return placed.reshape(tile_rows, tile_cols, width)


def solution(mesh):
    placed = (P("row", "col", None), P(), P(), P(), P(), P(), P())
    return jax.shard_map(
        body, mesh=mesh, in_specs=placed, out_specs=P("row", "col", None), check_vma=False
    )
```

```python
import functools
import math

import jax
import jax.numpy as jnp
from jax import lax
from jax.experimental import pallas as pl
from jax.experimental.pallas import tpu as pltpu
from jax.sharding import PartitionSpec as P

DILATION = 16
REACH = 6
HALO = 4
QUERY_ROWS = 8
MASKED = -1e30
LOG2E = 1.4426950408889634
VMEM_BYTES = 56 * 1024 * 1024


def layer_norm(values, gain):
    values_f = values.astype(jnp.float32)
    mean_value = jnp.mean(values_f, axis=-1, keepdims=True)
    centred = values_f - mean_value
    variance = jnp.mean(centred * centred, axis=-1, keepdims=True)
    return (centred * lax.rsqrt(variance + 1e-05) * gain).astype(jnp.bfloat16)


def dot(left, right):
    return jnp.dot(left, right, preferred_element_type=jnp.float32)


def fill_bias(rel_ref, rows_ref, full_ref, q_rows, k_rows, row_off, k_cols, col_places, first_key, groups):
    heads, entries = rel_ref.shape
    classes = math.isqrt(entries)
    q_cols = rows_ref.shape[1] // heads
    extent = q_rows + k_rows - 1
    before = q_rows - 1 + row_off - REACH
    chunks = -(-extent * k_cols // 128)
    width = chunks * 128
    place = lax.broadcasted_iota(jnp.int32, (1, width), 1)
    entry = lax.broadcasted_iota(jnp.int32, (entries, 1), 0)
    across = place // k_cols
    key_col = col_places(place - across * k_cols)
    down = across - before
    table = rel_ref[...] * LOG2E
    for j in range(q_cols):
        over = key_col - j + REACH
        known = (down >= 0) & (down < classes) & (over >= 0) & (over < classes)
        target = jnp.where(known, down * classes + over, -1)
        hot = (entry == target).astype(jnp.float32)
        found = jnp.dot(
            table, hot, precision=lax.Precision.HIGHEST, preferred_element_type=jnp.float32
        )
        for c in range(chunks):
            rows_ref[c, j * heads : (j + 1) * heads, :] = found[:, c * 128 : (c + 1) * 128]
    n_key = k_rows * k_cols
    for n in range(heads):
        strips = jnp.concatenate(
            [rows_ref[c, pl.ds(n, q_cols, stride=heads), :] for c in range(chunks)], axis=1
        )
        for i in range(q_rows):
            start = (q_rows - 1 - i) * k_cols
            strip = jnp.concatenate([strips[:, start : start + n_key]] * groups, axis=1)
            for t in range(groups):
                first = t * n_key + i * q_cols
                full_ref[n, first : first + q_cols, first_key : first_key + groups * n_key] = strip


def slot_places(index, shape):
    tile_cols, residue_rows, residue_cols, block_rows, block_cols, col_count, slot = shape
    row = index // tile_cols
    col = index - row * tile_cols
    row_block = row // DILATION
    col_block = col // DILATION
    row, col = row - row_block * DILATION, col - col_block * DILATION
    peer_row = row // residue_rows
    peer_col = col // residue_cols
    inner = (row - peer_row * residue_rows) * residue_cols + col - peer_col * residue_cols
    inner = (inner * block_rows + row_block) * block_cols + col_block
    return (peer_row * col_count + peer_col) * slot + inner


def group_places(index, shape):
    _, residue_rows, residue_cols, block_rows, block_cols, col_count, slot, row_count = shape
    used = residue_rows * residue_cols * block_rows * block_cols
    peer = index // slot
    inner = index - peer * slot
    peer_row = peer // col_count
    peer_col = peer - peer_row * col_count
    rest = inner // block_cols
    col_block = inner - rest * block_cols
    residue = rest // block_rows
    row_block = rest - residue * block_rows
    place = residue * (block_rows * row_count) + peer_row * block_rows + row_block
    place = place * (block_cols * col_count) + peer_col * block_cols + col_block
    return jnp.where(inner < used, place, -1)


def column(count):
    return lax.broadcasted_iota(jnp.int32, (count, 1), 0)


def line(count):
    return lax.broadcasted_iota(jnp.int32, (1, count), 1)


def one_hot(left, right):
    return jnp.where(left == right, 1.0, 0.0).astype(jnp.bfloat16)


def in_window(query, key, extent):
    start = jnp.clip(query - 3, 0, extent - 7)
    return (key >= start) & (key < start + 7)


def head_lanes(lanes, head_size):
    lane = lax.broadcasted_iota(jnp.int32, (1, lanes), 1)
    return [(lane // head_size) == h for h in range(lanes // head_size)]


def attend(queries, keys, values, bias, mask, head_size):
    count, lanes = queries.shape
    picks = head_lanes(lanes, head_size)
    zero = jnp.zeros_like(queries)
    stacked = jnp.concatenate([jnp.where(pick, queries, zero) for pick in picks], axis=0)
    scores = lax.dot_general(
        stacked, keys, (((1,), (1,)), ((), ())), preferred_element_type=jnp.float32
    )
    scores = scores.reshape(len(picks), count, keys.shape[0]) + bias
    if mask is not None:
        scores = scores + mask[None]
    peak = jnp.max(scores, axis=-1, keepdims=True)
    weights = jnp.exp2(scores - peak).astype(jnp.bfloat16)
    wide = jnp.concatenate([values, jnp.ones_like(values)], axis=1)
    summed = dot(weights.reshape(len(picks) * count, keys.shape[0]), wide)
    ratio = summed[:, :lanes] / summed[:, lanes:]
    result = ratio[:count]
    for h in range(1, len(picks)):
        result = jnp.where(picks[h], ratio[h * count : (h + 1) * count], result)
    return result.astype(jnp.bfloat16)


def finish(attended, stream, gain, proj_ref, up_ref, down_ref):
    hidden_width = up_ref.shape[1]
    part = math.gcd(hidden_width, 512)
    mixed = (dot(attended, proj_ref[...]) + stream.astype(jnp.float32)).astype(jnp.bfloat16)
    normed = layer_norm(mixed, gain)
    total = mixed.astype(jnp.float32)
    for first in range(0, hidden_width, part):
        hidden = jax.nn.gelu(dot(normed, up_ref[:, first : first + part]), approximate=True)
        total = total + dot(hidden.astype(jnp.bfloat16), down_ref[first : first + part, :])
    return total.astype(jnp.bfloat16)


def project(src_ref, gain, weight, dst_ref, scale, spans):
    for first, last in spans:
        result = dot(layer_norm(src_ref[first:last, :], gain), weight)
        if scale is not None:
            result = result * scale
        dst_ref[first:last, :] = result.astype(jnp.bfloat16)


def both_layers(
    geometry, x_ref, gains_ref, rel_ref, qkv_hbm, proj_hbm, up_hbm, down_hbm, out_ref,
    qkv_all, proj_all, up_all, down_all, q_ref, kv_ref, pad_ref, edge_ref, full_ref, full_two_ref,
    bias_ref, bias_two_ref, att_ref, att_two_ref, send_ref, arrive_ref, x_two_ref, reply_ref, back_ref,
    weight_sem, halo_send, halo_recv, go_send, go_recv, back_send, back_recv,
):
    row_count, col_count, tile_rows, tile_cols, heads, pack, places = geometry
    _, residue_rows, residue_cols, block_rows, block_cols, _, slot, _ = places
    tokens, width = x_ref.shape
    peers = row_count * col_count
    map_rows, map_cols = tile_rows * row_count, tile_cols * col_count
    group_rows, group_cols = block_rows * row_count, block_cols * col_count
    head_size = width // heads
    lanes = 128
    per = lanes // head_size
    scale = head_size ** (-0.5) * LOG2E
    my_row, my_col = lax.axis_index("row"), lax.axis_index("col")
    me = my_row * col_count + my_col

    def weight_copy(index, layer):
        src, dst = (
            (qkv_hbm, qkv_all), (proj_hbm, proj_all), (up_hbm, up_all), (down_hbm, down_all)
        )[index]
        return pltpu.make_async_copy(src.at[layer], dst.at[layer], weight_sem.at[index, layer])

    for layer in range(2):
        for index in range(4):
            weight_copy(index, layer).start()

    rim = HALO * tile_cols
    side = (tile_rows + 2 * HALO) * HALO
    own = tokens + 2 * rim
    corner = HALO * HALO
    edge = tile_rows * HALO
    pad_ref[0:rim, :] = jnp.zeros((rim, width), jnp.bfloat16)
    pad_ref[rim + tokens :, :] = jnp.zeros((rim + 2 * side, width), jnp.bfloat16)
    place = column(edge)
    source = place // HALO * tile_cols + place - place // HALO * HALO
    edge_ref[0:edge, :] = dot(one_hot(source, line(tokens)), x_ref[...]).astype(jnp.bfloat16)
    edge_ref[edge : 2 * edge, :] = dot(
        one_hot(source + tile_cols - HALO, line(tokens)), x_ref[...]
    ).astype(jnp.bfloat16)

    barrier = pltpu.get_barrier_semaphore()

    def greet(peer, carry):
        @pl.when(peer != me)
        def _():
            pl.semaphore_signal(
                barrier,
                inc=1,
                device_id=(peer // col_count, peer % col_count),
                device_id_type=pl.DeviceIdType.MESH,
            )

        return carry

    lax.fori_loop(0, peers, greet, 0)
    pl.semaphore_wait(barrier, peers - 1)

    left, right = own, own + side
    moves = (
        (-1, 0, x_ref, 0, rim + tokens, rim),
        (1, 0, x_ref, tokens - rim, 0, rim),
        (0, 1, edge_ref, edge, left + corner, edge),
        (0, -1, edge_ref, 0, right + corner, edge),
        (-1, 1, edge_ref, edge, left + corner + edge, corner),
        (-1, -1, edge_ref, 0, right + corner + edge, corner),
        (1, 1, edge_ref, 2 * edge - corner, left, corner),
        (1, -1, edge_ref, edge - corner, right, corner),
    )

    def exists(down, over):
        row, col = my_row + down, my_col + over
        return (row >= 0) & (row < row_count) & (col >= 0) & (col < col_count)

    def halo_copy(k):
        down, over, src, first, there, rows = moves[k]
        return pltpu.make_async_remote_copy(
            src_ref=src.at[first : first + rows],
            dst_ref=pad_ref.at[there : there + rows],
            send_sem=halo_send.at[k],
            recv_sem=halo_recv.at[k],
            device_id=(my_row + down, my_col + over),
            device_id_type=pl.DeviceIdType.MESH,
        )

    for k in range(len(moves)):

        @pl.when(exists(moves[k][0], moves[k][1]))
        def _(k=k):
            halo_copy(k).start()

    pad_ref[rim : rim + tokens, :] = x_ref[...]
    key_rows = QUERY_ROWS + 2 * HALO
    n_query = QUERY_ROWS * tile_cols
    sets = (
        (0, tile_cols, 0, lambda col: col),
        (own, HALO, key_rows * tile_cols, lambda col: col - HALO),
        (own + side, HALO, key_rows * (tile_cols + HALO), lambda col: col + tile_cols),
    )
    for _, k_cols, first_key, col_places in sets:
        fill_bias(
            rel_ref.at[0], bias_ref, full_ref, QUERY_ROWS, key_rows, HALO, k_cols, col_places,
            first_key, 1,
        )
    gain = gains_ref[0:1, :]
    weight_copy(0, 0).wait()
    project(x_ref, gain, qkv_all[0, :, :width], q_ref, scale, ((0, tokens),))
    kv_weight = qkv_all[0, :, width:]
    project(pad_ref, gain, kv_weight, kv_ref, None, ((rim, rim + tokens),))
    for k in range(len(moves)):

        @pl.when(exists(-moves[k][0], -moves[k][1]))
        def _(k=k):
            halo_copy(k).wait_recv()

    project(pad_ref, gain, kv_weight, kv_ref, None, ((0, rim), (rim + tokens, own + 2 * side)))

    first_row = my_row * tile_rows
    first_col = my_col * tile_cols
    query = column(n_query)
    query_row = query // tile_cols
    query_col = first_col + query - query_row * tile_cols
    seen_cols, key_row_list = [], []
    for _, k_cols, _, col_places in sets:
        key = line(key_rows * k_cols)
        key_row = key // k_cols
        key_row_list.append(key_row)
        key_col = first_col + col_places(key - key_row * k_cols)
        seen_cols.append(in_window(query_col, key_col, map_cols))
    for index in range(1, 4):
        weight_copy(index, 0).wait()

    def slot_rows(peer):
        return pl.ds(pl.multiple_of(peer * slot, slot), slot)

    def exchange(src, dst, send, recv, peer):
        return pltpu.make_async_remote_copy(
            src_ref=src.at[slot_rows(peer)],
            dst_ref=dst.at[slot_rows(me)],
            send_sem=send.at[peer],
            recv_sem=recv.at[me],
            device_id=(peer // col_count, peer % col_count),
            device_id_type=pl.DeviceIdType.MESH,
        )

    def send_slots(src, dst, send, recv, first, count):
        def one(p, carry):
            peer = first + (me + p) % count

            @pl.when(peer != me)
            def _():
                exchange(src, dst, send, recv, peer).start()

            @pl.when(peer == me)
            def _():
                dst[slot_rows(me), :] = src[slot_rows(me), :]

            return carry

        lax.fori_loop(0, count, one, 0)

    def wait_slots(src, dst, send, recv, sent):
        def one(peer, carry):
            @pl.when(peer != me)
            def _():
                if sent:
                    exchange(src, dst, send, recv, peer).wait_send()
                else:
                    pltpu.make_async_remote_copy(
                        src_ref=src.at[slot_rows(peer)],
                        dst_ref=dst.at[slot_rows(peer)],
                        send_sem=send.at[peer],
                        recv_sem=recv.at[peer],
                        device_id=(peer // col_count, peer % col_count),
                        device_id_type=pl.DeviceIdType.MESH,
                    ).wait_recv()

            return carry

        lax.fori_loop(0, peers, one, 0)

    halves = DILATION // QUERY_ROWS
    half_peers = peers // halves
    half_slots = half_peers * slot

    def half(h, carry):
        def step(k, inner):
            block = h + halves * k
            top = first_row + block * QUERY_ROWS
            masks = [
                jnp.where(
                    col_seen & in_window(top + query_row, top + key_row - HALO, map_rows), 0.0, MASKED
                )
                for col_seen, key_row in zip(seen_cols, key_row_list)
            ]
            mask = jnp.concatenate(masks, axis=1).astype(jnp.float32)
            q_rows = pl.ds(pl.multiple_of(block * n_query, n_query), n_query)
            to_rows = pl.ds(pl.multiple_of(k * n_query, n_query), n_query)
            k_rows = []
            for base, k_cols, _, _ in sets:
                stride = QUERY_ROWS * k_cols
                k_rows.append(pl.ds(pl.multiple_of(base + block * stride, 16), key_rows * k_cols))
            for g in range(width // lanes):
                cols = slice(g * lanes, (g + 1) * lanes)
                v_cols = slice(width + g * lanes, width + (g + 1) * lanes)
                att_ref[to_rows, cols] = attend(
                    q_ref[q_rows, cols],
                    jnp.concatenate([kv_ref[rows, cols] for rows in k_rows], axis=0),
                    jnp.concatenate([kv_ref[rows, v_cols] for rows in k_rows], axis=0),
                    full_ref[g * per : (g + 1) * per],
                    mask,
                    head_size,
                )
            return inner

        lax.fori_loop(0, block_rows, step, 0)
        blocks = [h + halves * k for k in range(block_rows)]
        stream = jnp.concatenate(
            [x_ref[pl.ds(pl.multiple_of(at * n_query, n_query), n_query), :] for at in blocks], axis=0
        )
        result = finish(
            att_ref[...], stream, gains_ref[1:2, :], proj_all.at[0], up_all.at[0], down_all.at[0]
        )
        here = line(block_rows * n_query)
        which = here // n_query
        token = (h + halves * which) * n_query + here - which * n_query
        hot = one_hot(h * half_slots + column(half_slots), slot_places(token, places[:7]))
        rows = pl.ds(pl.multiple_of(h * half_slots, half_slots), half_slots)
        send_ref[rows, :] = dot(hot, result).astype(jnp.bfloat16)
        send_slots(send_ref, arrive_ref, go_send, go_recv, h * half_peers, half_peers)
        return carry

    lax.fori_loop(0, halves, half, 0)

    size = group_rows * group_cols
    n_two = pack * size
    query, key = column(n_two), line(n_two)
    query_row, key_row = query // group_cols, key // group_cols
    query_col, key_col = query - query_row * group_cols, key - key_row * group_cols
    query_group, key_group = query // size, key // size
    seen = (
        (query_group == key_group)
        & in_window(query_row - query_group * group_rows, key_row - key_group * group_rows, group_rows)
        & in_window(query_col, key_col, group_cols)
    )
    fill_bias(
        rel_ref.at[1], bias_two_ref, full_two_ref, group_rows, group_rows, 0, group_cols,
        lambda col: col, 0, pack,
    )
    for n in range(heads):
        full_two_ref[n] = jnp.where(seen, full_two_ref[n], MASKED)
    for index in range(4):
        weight_copy(index, 1).wait()
    arrivals = peers * slot
    hot = one_hot(column(tokens), group_places(line(arrivals), places))
    wait_slots(send_ref, arrive_ref, go_send, go_recv, False)

    x_two_ref[...] = dot(hot, arrive_ref[...]).astype(jnp.bfloat16)
    gain = gains_ref[2:3, :]
    project(x_two_ref, gain, qkv_all[1, :, :width], q_ref, scale, ((0, tokens),))
    project(x_two_ref, gain, qkv_all[1, :, width:], kv_ref, None, ((0, tokens),))

    def step_two(block, carry):
        rows = pl.ds(pl.multiple_of(block * n_two, n_two), n_two)
        for g in range(width // lanes):
            cols = slice(g * lanes, (g + 1) * lanes)
            v_cols = slice(width + g * lanes, width + (g + 1) * lanes)
            att_two_ref[rows, cols] = attend(
                q_ref[rows, cols],
                kv_ref[rows, cols],
                kv_ref[rows, v_cols],
                full_two_ref[g * per : (g + 1) * per],
                None,
                head_size,
            )
        return carry

    lax.fori_loop(0, tokens // n_two, step_two, 0)

    def half_two(h, carry):
        rows = pl.ds(pl.multiple_of(h * half_slots, half_slots), half_slots)
        spots = group_places(h * half_slots + column(half_slots), places)
        attended = dot(one_hot(spots, line(tokens)), att_two_ref[...]).astype(jnp.bfloat16)
        reply_ref[rows, :] = finish(
            attended, arrive_ref[rows, :], gains_ref[3:4, :], proj_all.at[1], up_all.at[1], down_all.at[1]
        )
        send_slots(reply_ref, back_ref, back_send, back_recv, h * half_peers, half_peers)
        return carry

    lax.fori_loop(0, halves, half_two, 0)
    wait_slots(send_ref, arrive_ref, go_send, go_recv, True)
    for k in range(len(moves)):

        @pl.when(exists(moves[k][0], moves[k][1]))
        def _(k=k):
            halo_copy(k).wait_send()

    hot = one_hot(slot_places(column(tokens), places[:7]), line(arrivals))
    wait_slots(reply_ref, back_ref, back_send, back_recv, False)
    out_ref[...] = dot(hot, back_ref[...]).astype(jnp.bfloat16)
    wait_slots(reply_ref, back_ref, back_send, back_recv, True)


def body(tokens, norm_gains, qkv_weight, rel_bias, proj_weight, up_weight, down_weight):
    tile_rows, tile_cols, width = tokens.shape
    row_count = lax.axis_size("row")
    col_count = lax.axis_size("col")
    heads = rel_bias.shape[1]
    rel = rel_bias.reshape(rel_bias.shape[0], heads, -1)
    residue_rows = DILATION // row_count
    residue_cols = DILATION // col_count
    block_rows = tile_rows // DILATION
    block_cols = tile_cols // DILATION
    group_rows = block_rows * row_count
    group_cols = block_cols * col_count
    size = group_rows * group_cols
    pack = max(1, 128 // size)
    peers = row_count * col_count
    count = tile_rows * tile_cols
    slot = -(-(count // peers) // 16) * 16
    places = (
        tile_cols, residue_rows, residue_cols, block_rows, block_cols, col_count, slot, row_count
    )
    geometry = (row_count, col_count, tile_rows, tile_cols, heads, pack, places)
    key_rows = QUERY_ROWS + 2 * HALO
    n_query = QUERY_ROWS * tile_cols
    n_key = key_rows * (tile_cols + 2 * HALO)
    padded = count + 2 * HALO * tile_cols + 2 * HALO * (tile_rows + 2 * HALO)
    chunks = -(-(QUERY_ROWS + key_rows - 1) * tile_cols // 128)
    chunks_two = -(-(2 * group_rows - 1) * group_cols // 128)
    slots = peers * slot
    half = jnp.bfloat16
    weights = (qkv_weight, proj_weight, up_weight, down_weight)
    vmem = pl.BlockSpec(memory_space=pltpu.VMEM)
    hbm = pl.BlockSpec(memory_space=pl.ANY)
    result = pl.pallas_call(
        functools.partial(both_layers, geometry),
        out_shape=jax.ShapeDtypeStruct((count, width), half),
        in_specs=[vmem, vmem, vmem, hbm, hbm, hbm, hbm],
        out_specs=vmem,
        scratch_shapes=[pltpu.VMEM(weight.shape, weight.dtype) for weight in weights]
        + [
            pltpu.VMEM((count, width), half),
            pltpu.VMEM((padded, 2 * width), half),
            pltpu.VMEM((padded, width), half),
            pltpu.VMEM((2 * tile_rows * HALO, width), half),
            pltpu.VMEM((heads, n_query, n_key), jnp.float32),
            pltpu.VMEM((heads, pack * size, pack * size), jnp.float32),
            pltpu.VMEM((chunks, tile_cols * heads, 128), jnp.float32),
            pltpu.VMEM((chunks_two, group_cols * heads, 128), jnp.float32),
            pltpu.VMEM((block_rows * n_query, width), half),
            pltpu.VMEM((count, width), half),
            pltpu.VMEM((slots, width), half),
            pltpu.VMEM((slots, width), half),
            pltpu.VMEM((count, width), half),
            pltpu.VMEM((slots, width), half),
            pltpu.VMEM((slots, width), half),
            pltpu.SemaphoreType.DMA((4, 2)),
            pltpu.SemaphoreType.DMA((8,)),
            pltpu.SemaphoreType.DMA((8,)),
            pltpu.SemaphoreType.DMA((peers,)),
            pltpu.SemaphoreType.DMA((peers,)),
            pltpu.SemaphoreType.DMA((peers,)),
            pltpu.SemaphoreType.DMA((peers,)),
        ],
        compiler_params=pltpu.CompilerParams(
            collective_id=0, has_side_effects=True, vmem_limit_bytes=VMEM_BYTES
        ),
    )(tokens.reshape(count, width), norm_gains, rel, *weights)
    return result.reshape(tile_rows, tile_cols, width)


def solution(mesh):
    placed = (P("row", "col", None), P(), P(), P(), P(), P(), P())
    return jax.shard_map(
        body, mesh=mesh, in_specs=placed, out_specs=P("row", "col", None), check_vma=False
    )
```

```python
import functools
import math

import jax
import jax.numpy as jnp
from jax import lax
from jax.experimental import pallas as pl
from jax.experimental.pallas import tpu as pltpu
from jax.sharding import PartitionSpec as P

DILATION = 16
REACH = 6
HALO = 4
QUERY_ROWS = 8
MASKED = -1e30
LOG2E = 1.4426950408889634
VMEM_BYTES = 56 * 1024 * 1024


def layer_norm(values, gain):
    values_f = values.astype(jnp.float32)
    mean_value = jnp.mean(values_f, axis=-1, keepdims=True)
    centred = values_f - mean_value
    variance = jnp.mean(centred * centred, axis=-1, keepdims=True)
    return (centred * lax.rsqrt(variance + 1e-05) * gain).astype(jnp.bfloat16)


def dot(left, right):
    return jnp.dot(left, right, preferred_element_type=jnp.float32)


def fill_bias(rel_ref, rows_ref, full_ref, q_rows, k_rows, row_off, k_cols, col_places, first_key, groups):
    heads, classes, _ = rel_ref.shape
    entries = classes * classes
    q_cols = rows_ref.shape[1] // heads
    extent = q_rows + k_rows - 1
    before = q_rows - 1 + row_off - REACH
    chunks = -(-extent * k_cols // 128)
    width = chunks * 128
    place = lax.broadcasted_iota(jnp.int32, (1, width), 1)
    entry = lax.broadcasted_iota(jnp.int32, (entries, 1), 0)
    across = place // k_cols
    key_col = col_places(place - across * k_cols)
    down = across - before
    table = jnp.concatenate([rel_ref[:, dy, :] for dy in range(classes)], axis=1) * LOG2E
    parts = []
    for _ in range(3):
        parts.append(table.astype(jnp.bfloat16))
        table = table - parts[-1].astype(jnp.float32)
    stacked = jnp.concatenate(parts, axis=0)
    for j in range(q_cols):
        over = key_col - j + REACH
        known = (down >= 0) & (down < classes) & (over >= 0) & (over < classes)
        target = jnp.where(known, down * classes + over, -1)
        found = dot(stacked, one_hot(entry, target))
        found = found[:heads] + found[heads : 2 * heads] + found[2 * heads :]
        for c in range(chunks):
            rows_ref[c, j * heads : (j + 1) * heads, :] = found[:, c * 128 : (c + 1) * 128]
    n_key = k_rows * k_cols
    for n in range(heads):
        strips = jnp.concatenate(
            [rows_ref[c, pl.ds(n, q_cols, stride=heads), :] for c in range(chunks)], axis=1
        )
        for i in range(q_rows):
            start = (q_rows - 1 - i) * k_cols
            strip = jnp.concatenate([strips[:, start : start + n_key]] * groups, axis=1)
            for t in range(groups):
                first = t * n_key + i * q_cols
                full_ref[n, first : first + q_cols, first_key : first_key + groups * n_key] = strip


def slot_places(index, shape):
    tile_cols, residue_rows, residue_cols, block_rows, block_cols, col_count, slot = shape
    row = index // tile_cols
    col = index - row * tile_cols
    row_block = row // DILATION
    col_block = col // DILATION
    row, col = row - row_block * DILATION, col - col_block * DILATION
    peer_row = row // residue_rows
    peer_col = col // residue_cols
    inner = (row - peer_row * residue_rows) * residue_cols + col - peer_col * residue_cols
    inner = (inner * block_rows + row_block) * block_cols + col_block
    return (peer_row * col_count + peer_col) * slot + inner


def group_places(index, shape):
    _, residue_rows, residue_cols, block_rows, block_cols, col_count, slot, row_count = shape
    used = residue_rows * residue_cols * block_rows * block_cols
    peer = index // slot
    inner = index - peer * slot
    peer_row = peer // col_count
    peer_col = peer - peer_row * col_count
    rest = inner // block_cols
    col_block = inner - rest * block_cols
    residue = rest // block_rows
    row_block = rest - residue * block_rows
    place = residue * (block_rows * row_count) + peer_row * block_rows + row_block
    place = place * (block_cols * col_count) + peer_col * block_cols + col_block
    return jnp.where(inner < used, place, -1)


def column(count):
    return lax.broadcasted_iota(jnp.int32, (count, 1), 0)


def line(count):
    return lax.broadcasted_iota(jnp.int32, (1, count), 1)


def one_hot(left, right):
    return jnp.where(left == right, 1.0, 0.0).astype(jnp.bfloat16)


def in_window(query, key, extent):
    start = jnp.clip(query - 3, 0, extent - 7)
    return (key >= start) & (key < start + 7)


def head_lanes(lanes, head_size):
    lane = lax.broadcasted_iota(jnp.int32, (1, lanes), 1)
    return [(lane // head_size) == h for h in range(lanes // head_size)]


def attend(queries, keys, values, bias, mask, head_size):
    count, lanes = queries.shape
    picks = head_lanes(lanes, head_size)
    zero = jnp.zeros_like(queries)
    stacked = jnp.concatenate([jnp.where(pick, queries, zero) for pick in picks], axis=0)
    scores = lax.dot_general(
        stacked, keys, (((1,), (1,)), ((), ())), preferred_element_type=jnp.float32
    )
    scores = scores.reshape(len(picks), count, keys.shape[0]) + bias
    if mask is not None:
        scores = scores + mask[None]
    peak = jnp.max(scores, axis=-1, keepdims=True)
    weights = jnp.exp2(scores - peak).astype(jnp.bfloat16)
    wide = jnp.concatenate([values, jnp.ones_like(values)], axis=1)
    summed = dot(weights.reshape(len(picks) * count, keys.shape[0]), wide)
    ratio = summed[:, :lanes] / summed[:, lanes:]
    result = ratio[:count]
    for h in range(1, len(picks)):
        result = jnp.where(picks[h], ratio[h * count : (h + 1) * count], result)
    return result.astype(jnp.bfloat16)


def finish(attended, stream, gain, proj_ref, up_ref, down_ref):
    hidden_width = up_ref.shape[1]
    part = math.gcd(hidden_width, 512)
    mixed = (dot(attended, proj_ref[...]) + stream.astype(jnp.float32)).astype(jnp.bfloat16)
    normed = layer_norm(mixed, gain)
    total = mixed.astype(jnp.float32)
    for first in range(0, hidden_width, part):
        hidden = jax.nn.gelu(dot(normed, up_ref[:, first : first + part]), approximate=True)
        total = total + dot(hidden.astype(jnp.bfloat16), down_ref[first : first + part, :])
    return total.astype(jnp.bfloat16)


def project(src_ref, gain, weight, dst_ref, scale, spans):
    for first, last in spans:
        result = dot(layer_norm(src_ref[first:last, :], gain), weight)
        if scale is not None:
            result = result * scale
        dst_ref[first:last, :] = result.astype(jnp.bfloat16)


def both_layers(
    geometry, x_ref, gains_ref, rel_ref, qkv_hbm, proj_hbm, up_hbm, down_hbm, out_ref,
    qkv_all, proj_all, up_all, down_all, q_ref, kv_ref, pad_ref, edge_ref, full_ref, full_two_ref,
    bias_ref, bias_two_ref, att_ref, att_two_ref, send_ref, arrive_ref, x_two_ref, reply_ref, back_ref,
    weight_sem, halo_send, halo_recv, go_send, go_recv, back_send, back_recv,
):
    row_count, col_count, tile_rows, tile_cols, heads, pack, places = geometry
    _, residue_rows, residue_cols, block_rows, block_cols, _, slot, _ = places
    tokens, width = x_ref.shape
    peers = row_count * col_count
    map_rows, map_cols = tile_rows * row_count, tile_cols * col_count
    group_rows, group_cols = block_rows * row_count, block_cols * col_count
    head_size = width // heads
    lanes = 128
    per = lanes // head_size
    scale = head_size ** (-0.5) * LOG2E
    my_row, my_col = lax.axis_index("row"), lax.axis_index("col")
    me = my_row * col_count + my_col

    def weight_copy(index, layer):
        src, dst = (
            (qkv_hbm, qkv_all), (proj_hbm, proj_all), (up_hbm, up_all), (down_hbm, down_all)
        )[index]
        return pltpu.make_async_copy(src.at[layer], dst.at[layer], weight_sem.at[index, layer])

    for layer in range(2):
        for index in range(4):
            weight_copy(index, layer).start()

    rim = HALO * tile_cols
    side = (tile_rows + 2 * HALO) * HALO
    own = tokens + 2 * rim
    corner = HALO * HALO
    edge = tile_rows * HALO
    pad_ref[0:rim, :] = jnp.zeros((rim, width), jnp.bfloat16)
    pad_ref[rim + tokens :, :] = jnp.zeros((rim + 2 * side, width), jnp.bfloat16)
    place = column(edge)
    source = place // HALO * tile_cols + place - place // HALO * HALO
    edge_ref[0:edge, :] = dot(one_hot(source, line(tokens)), x_ref[...]).astype(jnp.bfloat16)
    edge_ref[edge : 2 * edge, :] = dot(
        one_hot(source + tile_cols - HALO, line(tokens)), x_ref[...]
    ).astype(jnp.bfloat16)

    barrier = pltpu.get_barrier_semaphore()

    def greet(peer, carry):
        @pl.when(peer != me)
        def _():
            pl.semaphore_signal(
                barrier,
                inc=1,
                device_id=(peer // col_count, peer % col_count),
                device_id_type=pl.DeviceIdType.MESH,
            )

        return carry

    lax.fori_loop(0, peers, greet, 0)
    pl.semaphore_wait(barrier, peers - 1)

    left, right = own, own + side
    moves = (
        (-1, 0, x_ref, 0, rim + tokens, rim),
        (1, 0, x_ref, tokens - rim, 0, rim),
        (0, 1, edge_ref, edge, left + corner, edge),
        (0, -1, edge_ref, 0, right + corner, edge),
        (-1, 1, edge_ref, edge, left + corner + edge, corner),
        (-1, -1, edge_ref, 0, right + corner + edge, corner),
        (1, 1, edge_ref, 2 * edge - corner, left, corner),
        (1, -1, edge_ref, edge - corner, right, corner),
    )

    def exists(down, over):
        row, col = my_row + down, my_col + over
        return (row >= 0) & (row < row_count) & (col >= 0) & (col < col_count)

    def halo_copy(k):
        down, over, src, first, there, rows = moves[k]
        return pltpu.make_async_remote_copy(
            src_ref=src.at[first : first + rows],
            dst_ref=pad_ref.at[there : there + rows],
            send_sem=halo_send.at[k],
            recv_sem=halo_recv.at[k],
            device_id=(my_row + down, my_col + over),
            device_id_type=pl.DeviceIdType.MESH,
        )

    for k in range(len(moves)):

        @pl.when(exists(moves[k][0], moves[k][1]))
        def _(k=k):
            halo_copy(k).start()

    pad_ref[rim : rim + tokens, :] = x_ref[...]
    key_rows = QUERY_ROWS + 2 * HALO
    n_query = QUERY_ROWS * tile_cols
    sets = (
        (0, tile_cols, 0, lambda col: col),
        (own, HALO, key_rows * tile_cols, lambda col: col - HALO),
        (own + side, HALO, key_rows * (tile_cols + HALO), lambda col: col + tile_cols),
    )
    for _, k_cols, first_key, col_places in sets:
        fill_bias(
            rel_ref.at[0], bias_ref, full_ref, QUERY_ROWS, key_rows, HALO, k_cols, col_places,
            first_key, 1,
        )
    gain = gains_ref[0:1, :]
    weight_copy(0, 0).wait()
    project(x_ref, gain, qkv_all[0, :, :width], q_ref, scale, ((0, tokens),))
    kv_weight = qkv_all[0, :, width:]
    project(pad_ref, gain, kv_weight, kv_ref, None, ((rim, rim + tokens),))
    for k in range(len(moves)):

        @pl.when(exists(-moves[k][0], -moves[k][1]))
        def _(k=k):
            halo_copy(k).wait_recv()

    project(pad_ref, gain, kv_weight, kv_ref, None, ((0, rim), (rim + tokens, own + 2 * side)))

    first_row = my_row * tile_rows
    first_col = my_col * tile_cols
    query = column(n_query)
    query_row = query // tile_cols
    query_col = first_col + query - query_row * tile_cols
    seen_cols, key_row_list = [], []
    for _, k_cols, _, col_places in sets:
        key = line(key_rows * k_cols)
        key_row = key // k_cols
        key_row_list.append(key_row)
        key_col = first_col + col_places(key - key_row * k_cols)
        seen_cols.append(in_window(query_col, key_col, map_cols))
    for index in range(1, 4):
        weight_copy(index, 0).wait()

    def slot_rows(peer):
        return pl.ds(pl.multiple_of(peer * slot, slot), slot)

    def exchange(src, dst, send, recv, peer):
        return pltpu.make_async_remote_copy(
            src_ref=src.at[slot_rows(peer)],
            dst_ref=dst.at[slot_rows(me)],
            send_sem=send.at[peer],
            recv_sem=recv.at[me],
            device_id=(peer // col_count, peer % col_count),
            device_id_type=pl.DeviceIdType.MESH,
        )

    def send_slots(src, dst, send, recv, first, count):
        def one(p, carry):
            peer = first + (me + p) % count

            @pl.when(peer != me)
            def _():
                exchange(src, dst, send, recv, peer).start()

            @pl.when(peer == me)
            def _():
                dst[slot_rows(me), :] = src[slot_rows(me), :]

            return carry

        lax.fori_loop(0, count, one, 0)

    def wait_slots(src, dst, send, recv, sent):
        def one(peer, carry):
            @pl.when(peer != me)
            def _():
                if sent:
                    exchange(src, dst, send, recv, peer).wait_send()
                else:
                    pltpu.make_async_remote_copy(
                        src_ref=src.at[slot_rows(peer)],
                        dst_ref=dst.at[slot_rows(peer)],
                        send_sem=send.at[peer],
                        recv_sem=recv.at[peer],
                        device_id=(peer // col_count, peer % col_count),
                        device_id_type=pl.DeviceIdType.MESH,
                    ).wait_recv()

            return carry

        lax.fori_loop(0, peers, one, 0)

    halves = DILATION // QUERY_ROWS
    half_peers = peers // halves
    half_slots = half_peers * slot

    def half(turn, carry):
        h = (turn + my_col) % halves

        def step(k, inner):
            block = h + halves * k
            top = first_row + block * QUERY_ROWS
            masks = [
                jnp.where(
                    col_seen & in_window(top + query_row, top + key_row - HALO, map_rows), 0.0, MASKED
                )
                for col_seen, key_row in zip(seen_cols, key_row_list)
            ]
            mask = jnp.concatenate(masks, axis=1).astype(jnp.float32)
            q_rows = pl.ds(pl.multiple_of(block * n_query, n_query), n_query)
            to_rows = pl.ds(pl.multiple_of(k * n_query, n_query), n_query)
            k_rows = []
            for base, k_cols, _, _ in sets:
                stride = QUERY_ROWS * k_cols
                k_rows.append(pl.ds(pl.multiple_of(base + block * stride, 16), key_rows * k_cols))
            for g in range(width // lanes):
                cols = slice(g * lanes, (g + 1) * lanes)
                v_cols = slice(width + g * lanes, width + (g + 1) * lanes)
                att_ref[to_rows, cols] = attend(
                    q_ref[q_rows, cols],
                    jnp.concatenate([kv_ref[rows, cols] for rows in k_rows], axis=0),
                    jnp.concatenate([kv_ref[rows, v_cols] for rows in k_rows], axis=0),
                    full_ref[g * per : (g + 1) * per],
                    mask,
                    head_size,
                )
            return inner

        lax.fori_loop(0, block_rows, step, 0)
        blocks = [h + halves * k for k in range(block_rows)]
        stream = jnp.concatenate(
            [x_ref[pl.ds(pl.multiple_of(at * n_query, n_query), n_query), :] for at in blocks], axis=0
        )
        result = finish(
            att_ref[...], stream, gains_ref[1:2, :], proj_all.at[0], up_all.at[0], down_all.at[0]
        )
        here = line(block_rows * n_query)
        which = here // n_query
        token = (h + halves * which) * n_query + here - which * n_query
        hot = one_hot(h * half_slots + column(half_slots), slot_places(token, places[:7]))
        rows = pl.ds(pl.multiple_of(h * half_slots, half_slots), half_slots)
        send_ref[rows, :] = dot(hot, result).astype(jnp.bfloat16)
        send_slots(send_ref, arrive_ref, go_send, go_recv, h * half_peers, half_peers)
        return carry

    lax.fori_loop(0, halves, half, 0)

    size = group_rows * group_cols
    n_two = pack * size
    query, key = column(n_two), line(n_two)
    query_row, key_row = query // group_cols, key // group_cols
    query_col, key_col = query - query_row * group_cols, key - key_row * group_cols
    query_group, key_group = query // size, key // size
    seen = (
        (query_group == key_group)
        & in_window(query_row - query_group * group_rows, key_row - key_group * group_rows, group_rows)
        & in_window(query_col, key_col, group_cols)
    )
    fill_bias(
        rel_ref.at[1], bias_two_ref, full_two_ref, group_rows, group_rows, 0, group_cols,
        lambda col: col, 0, pack,
    )
    for n in range(heads):
        full_two_ref[n] = jnp.where(seen, full_two_ref[n], MASKED)
    for index in range(4):
        weight_copy(index, 1).wait()
    arrivals = peers * slot
    hot = one_hot(column(tokens), group_places(line(arrivals), places))
    wait_slots(send_ref, arrive_ref, go_send, go_recv, False)

    x_two_ref[...] = dot(hot, arrive_ref[...]).astype(jnp.bfloat16)
    gain = gains_ref[2:3, :]
    project(x_two_ref, gain, qkv_all[1, :, :width], q_ref, scale, ((0, tokens),))
    project(x_two_ref, gain, qkv_all[1, :, width:], kv_ref, None, ((0, tokens),))

    def step_two(block, carry):
        rows = pl.ds(pl.multiple_of(block * n_two, n_two), n_two)
        for g in range(width // lanes):
            cols = slice(g * lanes, (g + 1) * lanes)
            v_cols = slice(width + g * lanes, width + (g + 1) * lanes)
            att_two_ref[rows, cols] = attend(
                q_ref[rows, cols],
                kv_ref[rows, cols],
                kv_ref[rows, v_cols],
                full_two_ref[g * per : (g + 1) * per],
                None,
                head_size,
            )
        return carry

    lax.fori_loop(0, tokens // n_two, step_two, 0)

    def half_two(turn, carry):
        h = (turn + my_col) % halves
        rows = pl.ds(pl.multiple_of(h * half_slots, half_slots), half_slots)
        spots = group_places(h * half_slots + column(half_slots), places)
        attended = dot(one_hot(spots, line(tokens)), att_two_ref[...]).astype(jnp.bfloat16)
        reply_ref[rows, :] = finish(
            attended, arrive_ref[rows, :], gains_ref[3:4, :], proj_all.at[1], up_all.at[1], down_all.at[1]
        )
        send_slots(reply_ref, back_ref, back_send, back_recv, h * half_peers, half_peers)
        return carry

    lax.fori_loop(0, halves, half_two, 0)
    wait_slots(send_ref, arrive_ref, go_send, go_recv, True)
    for k in range(len(moves)):

        @pl.when(exists(moves[k][0], moves[k][1]))
        def _(k=k):
            halo_copy(k).wait_send()

    hot = one_hot(slot_places(column(tokens), places[:7]), line(arrivals))
    wait_slots(reply_ref, back_ref, back_send, back_recv, False)
    out_ref[...] = dot(hot, back_ref[...]).astype(jnp.bfloat16)
    wait_slots(reply_ref, back_ref, back_send, back_recv, True)


def body(tokens, norm_gains, qkv_weight, rel_bias, proj_weight, up_weight, down_weight):
    tile_rows, tile_cols, width = tokens.shape
    row_count = lax.axis_size("row")
    col_count = lax.axis_size("col")
    heads = rel_bias.shape[1]
    residue_rows = DILATION // row_count
    residue_cols = DILATION // col_count
    block_rows = tile_rows // DILATION
    block_cols = tile_cols // DILATION
    group_rows = block_rows * row_count
    group_cols = block_cols * col_count
    size = group_rows * group_cols
    pack = max(1, 128 // size)
    peers = row_count * col_count
    count = tile_rows * tile_cols
    slot = -(-(count // peers) // 16) * 16
    places = (
        tile_cols, residue_rows, residue_cols, block_rows, block_cols, col_count, slot, row_count
    )
    geometry = (row_count, col_count, tile_rows, tile_cols, heads, pack, places)
    key_rows = QUERY_ROWS + 2 * HALO
    n_query = QUERY_ROWS * tile_cols
    n_key = key_rows * (tile_cols + 2 * HALO)
    padded = count + 2 * HALO * tile_cols + 2 * HALO * (tile_rows + 2 * HALO)
    chunks = -(-(QUERY_ROWS + key_rows - 1) * tile_cols // 128)
    chunks_two = -(-(2 * group_rows - 1) * group_cols // 128)
    slots = peers * slot
    half = jnp.bfloat16
    weights = (qkv_weight, proj_weight, up_weight, down_weight)
    vmem = pl.BlockSpec(memory_space=pltpu.VMEM)
    hbm = pl.BlockSpec(memory_space=pl.ANY)
    result = pl.pallas_call(
        functools.partial(both_layers, geometry),
        out_shape=jax.ShapeDtypeStruct((count, width), half),
        in_specs=[vmem, vmem, vmem, hbm, hbm, hbm, hbm],
        out_specs=vmem,
        scratch_shapes=[pltpu.VMEM(weight.shape, weight.dtype) for weight in weights]
        + [
            pltpu.VMEM((count, width), half),
            pltpu.VMEM((padded, 2 * width), half),
            pltpu.VMEM((padded, width), half),
            pltpu.VMEM((2 * tile_rows * HALO, width), half),
            pltpu.VMEM((heads, n_query, n_key), jnp.float32),
            pltpu.VMEM((heads, pack * size, pack * size), jnp.float32),
            pltpu.VMEM((chunks, tile_cols * heads, 128), jnp.float32),
            pltpu.VMEM((chunks_two, group_cols * heads, 128), jnp.float32),
            pltpu.VMEM((block_rows * n_query, width), half),
            pltpu.VMEM((count, width), half),
            pltpu.VMEM((slots, width), half),
            pltpu.VMEM((slots, width), half),
            pltpu.VMEM((count, width), half),
            pltpu.VMEM((slots, width), half),
            pltpu.VMEM((slots, width), half),
            pltpu.SemaphoreType.DMA((4, 2)),
            pltpu.SemaphoreType.DMA((8,)),
            pltpu.SemaphoreType.DMA((8,)),
            pltpu.SemaphoreType.DMA((peers,)),
            pltpu.SemaphoreType.DMA((peers,)),
            pltpu.SemaphoreType.DMA((peers,)),
            pltpu.SemaphoreType.DMA((peers,)),
        ],
        compiler_params=pltpu.CompilerParams(
            collective_id=0, has_side_effects=True, vmem_limit_bytes=VMEM_BYTES
        ),
    )(tokens.reshape(count, width), norm_gains, rel_bias, *weights)
    return result.reshape(tile_rows, tile_cols, width)


def solution(mesh):
    placed = (P("row", "col", None), P(), P(), P(), P(), P(), P())
    return jax.shard_map(
        body, mesh=mesh, in_specs=placed, out_specs=P("row", "col", None), check_vma=False
    )
```

```python
import functools
import math

import jax
import jax.numpy as jnp
from jax import lax
from jax.experimental import pallas as pl
from jax.experimental.pallas import tpu as pltpu
from jax.sharding import PartitionSpec as P

DILATION = 16
REACH = 6
HALO = 4
QUERY_ROWS = 8
MASKED = -1e30
LOG2E = 1.4426950408889634
VMEM_BYTES = 56 * 1024 * 1024


def layer_norm(values, gain):
    values_f = values.astype(jnp.float32)
    mean_value = jnp.mean(values_f, axis=-1, keepdims=True)
    centred = values_f - mean_value
    variance = jnp.mean(centred * centred, axis=-1, keepdims=True)
    return (centred * lax.rsqrt(variance + 1e-05) * gain).astype(jnp.bfloat16)


def dot(left, right):
    return jnp.dot(left, right, preferred_element_type=jnp.float32)


def fill_bias(rel_ref, rows_ref, full_ref, q_rows, k_rows, row_off, k_cols, col_places, first_key, groups):
    classes, _, heads = rel_ref.shape
    entries = classes * classes
    q_cols = rows_ref.shape[1] // heads
    extent = q_rows + k_rows - 1
    before = q_rows - 1 + row_off - REACH
    chunks = -(-extent * k_cols // 128)
    width = chunks * 128
    place = lax.broadcasted_iota(jnp.int32, (1, width), 1)
    entry = lax.broadcasted_iota(jnp.int32, (entries, 1), 0)
    across = place // k_cols
    key_col = col_places(place - across * k_cols)
    down = across - before
    table = jnp.concatenate([rel_ref[dy] for dy in range(classes)], axis=0) * LOG2E
    parts = []
    for _ in range(3):
        parts.append(table.astype(jnp.bfloat16))
        table = table - parts[-1].astype(jnp.float32)
    stacked = jnp.concatenate([part.T for part in parts], axis=0)
    for j in range(q_cols):
        over = key_col - j + REACH
        known = (down >= 0) & (down < classes) & (over >= 0) & (over < classes)
        target = jnp.where(known, down * classes + over, -1)
        found = dot(stacked, one_hot(entry, target))
        found = found[:heads] + found[heads : 2 * heads] + found[2 * heads :]
        for c in range(chunks):
            rows_ref[c, j * heads : (j + 1) * heads, :] = found[:, c * 128 : (c + 1) * 128]
    n_key = k_rows * k_cols
    for n in range(heads):
        strips = jnp.concatenate(
            [rows_ref[c, pl.ds(n, q_cols, stride=heads), :] for c in range(chunks)], axis=1
        )
        for i in range(q_rows):
            start = (q_rows - 1 - i) * k_cols
            strip = jnp.concatenate([strips[:, start : start + n_key]] * groups, axis=1)
            for t in range(groups):
                first = t * n_key + i * q_cols
                full_ref[n, first : first + q_cols, first_key : first_key + groups * n_key] = strip


def slot_places(index, shape):
    tile_cols, residue_rows, residue_cols, block_rows, block_cols, col_count, slot = shape
    row = index // tile_cols
    col = index - row * tile_cols
    row_block = row // DILATION
    col_block = col // DILATION
    row, col = row - row_block * DILATION, col - col_block * DILATION
    peer_row = row // residue_rows
    peer_col = col // residue_cols
    inner = (row - peer_row * residue_rows) * residue_cols + col - peer_col * residue_cols
    inner = (inner * block_rows + row_block) * block_cols + col_block
    return (peer_row * col_count + peer_col) * slot + inner


def group_places(index, shape):
    _, residue_rows, residue_cols, block_rows, block_cols, col_count, slot, row_count = shape
    used = residue_rows * residue_cols * block_rows * block_cols
    peer = index // slot
    inner = index - peer * slot
    peer_row = peer // col_count
    peer_col = peer - peer_row * col_count
    rest = inner // block_cols
    col_block = inner - rest * block_cols
    residue = rest // block_rows
    row_block = rest - residue * block_rows
    place = residue * (block_rows * row_count) + peer_row * block_rows + row_block
    place = place * (block_cols * col_count) + peer_col * block_cols + col_block
    return jnp.where(inner < used, place, -1)


def column(count):
    return lax.broadcasted_iota(jnp.int32, (count, 1), 0)


def line(count):
    return lax.broadcasted_iota(jnp.int32, (1, count), 1)


def one_hot(left, right):
    return jnp.where(left == right, 1.0, 0.0).astype(jnp.bfloat16)


def in_window(query, key, extent):
    start = jnp.clip(query - 3, 0, extent - 7)
    return (key >= start) & (key < start + 7)


def head_lanes(lanes, head_size):
    lane = lax.broadcasted_iota(jnp.int32, (1, lanes), 1)
    return [(lane // head_size) == h for h in range(lanes // head_size)]


def attend(queries, keys, values, bias, mask, head_size):
    count, lanes = queries.shape
    picks = head_lanes(lanes, head_size)
    zero = jnp.zeros_like(queries)
    stacked = jnp.concatenate([jnp.where(pick, queries, zero) for pick in picks], axis=0)
    scores = lax.dot_general(
        stacked, keys, (((1,), (1,)), ((), ())), preferred_element_type=jnp.float32
    )
    scores = scores.reshape(len(picks), count, keys.shape[0]) + bias
    if mask is not None:
        scores = scores + mask[None]
    peak = jnp.max(scores, axis=-1, keepdims=True)
    weights = jnp.exp2(scores - peak).astype(jnp.bfloat16)
    wide = jnp.concatenate([values, jnp.ones_like(values)], axis=1)
    summed = dot(weights.reshape(len(picks) * count, keys.shape[0]), wide)
    ratio = summed[:, :lanes] / summed[:, lanes:]
    result = ratio[:count]
    for h in range(1, len(picks)):
        result = jnp.where(picks[h], ratio[h * count : (h + 1) * count], result)
    return result.astype(jnp.bfloat16)


def finish(attended, stream, gain, proj_ref, up_ref, down_ref):
    hidden_width = up_ref.shape[1]
    part = math.gcd(hidden_width, 512)
    mixed = (dot(attended, proj_ref[...]) + stream.astype(jnp.float32)).astype(jnp.bfloat16)
    normed = layer_norm(mixed, gain)
    total = mixed.astype(jnp.float32)
    for first in range(0, hidden_width, part):
        hidden = jax.nn.gelu(dot(normed, up_ref[:, first : first + part]), approximate=True)
        total = total + dot(hidden.astype(jnp.bfloat16), down_ref[first : first + part, :])
    return total.astype(jnp.bfloat16)


def project(src_ref, gain, weight, dst_ref, scale, spans):
    for first, last in spans:
        result = dot(layer_norm(src_ref[first:last, :], gain), weight)
        if scale is not None:
            result = result * scale
        dst_ref[first:last, :] = result.astype(jnp.bfloat16)


def both_layers(
    geometry, x_ref, gains_ref, rel_ref, qkv_hbm, proj_hbm, up_hbm, down_hbm, out_ref,
    qkv_all, proj_all, up_all, down_all, q_ref, kv_ref, pad_ref, edge_ref, full_ref, full_two_ref,
    bias_ref, bias_two_ref, att_ref, att_two_ref, send_ref, arrive_ref, x_two_ref, reply_ref, back_ref,
    weight_sem, halo_send, halo_recv, go_send, go_recv, back_send, back_recv,
):
    row_count, col_count, tile_rows, tile_cols, heads, pack, places = geometry
    _, residue_rows, residue_cols, block_rows, block_cols, _, slot, _ = places
    tokens, width = x_ref.shape
    peers = row_count * col_count
    map_rows, map_cols = tile_rows * row_count, tile_cols * col_count
    group_rows, group_cols = block_rows * row_count, block_cols * col_count
    head_size = width // heads
    lanes = 128
    per = lanes // head_size
    scale = head_size ** (-0.5) * LOG2E
    my_row, my_col = lax.axis_index("row"), lax.axis_index("col")
    me = my_row * col_count + my_col

    def weight_copy(index, layer):
        src, dst = (
            (qkv_hbm, qkv_all), (proj_hbm, proj_all), (up_hbm, up_all), (down_hbm, down_all)
        )[index]
        return pltpu.make_async_copy(src.at[layer], dst.at[layer], weight_sem.at[index, layer])

    for layer in range(2):
        for index in range(4):
            weight_copy(index, layer).start()

    rim = HALO * tile_cols
    side = (tile_rows + 2 * HALO) * HALO
    own = tokens + 2 * rim
    corner = HALO * HALO
    edge = tile_rows * HALO
    pad_ref[0:rim, :] = jnp.zeros((rim, width), jnp.bfloat16)
    pad_ref[rim + tokens :, :] = jnp.zeros((rim + 2 * side, width), jnp.bfloat16)
    place = column(edge)
    source = place // HALO * tile_cols + place - place // HALO * HALO
    edge_ref[0:edge, :] = dot(one_hot(source, line(tokens)), x_ref[...]).astype(jnp.bfloat16)
    edge_ref[edge : 2 * edge, :] = dot(
        one_hot(source + tile_cols - HALO, line(tokens)), x_ref[...]
    ).astype(jnp.bfloat16)

    barrier = pltpu.get_barrier_semaphore()

    def greet(peer, carry):
        @pl.when(peer != me)
        def _():
            pl.semaphore_signal(
                barrier,
                inc=1,
                device_id=(peer // col_count, peer % col_count),
                device_id_type=pl.DeviceIdType.MESH,
            )

        return carry

    lax.fori_loop(0, peers, greet, 0)
    key_rows = QUERY_ROWS + 2 * HALO
    n_query = QUERY_ROWS * tile_cols
    sets = (
        (0, tile_cols, 0, lambda col: col),
        (own, HALO, key_rows * tile_cols, lambda col: col - HALO),
        (own + side, HALO, key_rows * (tile_cols + HALO), lambda col: col + tile_cols),
    )
    fill_bias(
        rel_ref.at[:, :, 0], bias_ref, full_ref, QUERY_ROWS, key_rows, HALO, tile_cols, sets[0][3], 0, 1
    )
    pl.semaphore_wait(barrier, peers - 1)

    left, right = own, own + side
    moves = (
        (-1, 0, x_ref, 0, rim + tokens, rim),
        (1, 0, x_ref, tokens - rim, 0, rim),
        (0, 1, edge_ref, edge, left + corner, edge),
        (0, -1, edge_ref, 0, right + corner, edge),
        (-1, 1, edge_ref, edge, left + corner + edge, corner),
        (-1, -1, edge_ref, 0, right + corner + edge, corner),
        (1, 1, edge_ref, 2 * edge - corner, left, corner),
        (1, -1, edge_ref, edge - corner, right, corner),
    )

    def exists(down, over):
        row, col = my_row + down, my_col + over
        return (row >= 0) & (row < row_count) & (col >= 0) & (col < col_count)

    def halo_copy(k):
        down, over, src, first, there, rows = moves[k]
        return pltpu.make_async_remote_copy(
            src_ref=src.at[first : first + rows],
            dst_ref=pad_ref.at[there : there + rows],
            send_sem=halo_send.at[k],
            recv_sem=halo_recv.at[k],
            device_id=(my_row + down, my_col + over),
            device_id_type=pl.DeviceIdType.MESH,
        )

    for k in range(len(moves)):

        @pl.when(exists(moves[k][0], moves[k][1]))
        def _(k=k):
            halo_copy(k).start()

    pad_ref[rim : rim + tokens, :] = x_ref[...]
    for _, k_cols, first_key, col_places in sets[1:]:
        fill_bias(
            rel_ref.at[:, :, 0], bias_ref, full_ref, QUERY_ROWS, key_rows, HALO, k_cols, col_places,
            first_key, 1,
        )
    gain = gains_ref[0:1, :]
    weight_copy(0, 0).wait()
    project(x_ref, gain, qkv_all[0, :, :width], q_ref, scale, ((0, tokens),))
    kv_weight = qkv_all[0, :, width:]
    project(pad_ref, gain, kv_weight, kv_ref, None, ((rim, rim + tokens),))
    for k in range(len(moves)):

        @pl.when(exists(-moves[k][0], -moves[k][1]))
        def _(k=k):
            halo_copy(k).wait_recv()

    project(pad_ref, gain, kv_weight, kv_ref, None, ((0, rim), (rim + tokens, own + 2 * side)))

    first_row = my_row * tile_rows
    first_col = my_col * tile_cols
    query = column(n_query)
    query_row = query // tile_cols
    query_col = first_col + query - query_row * tile_cols
    seen_cols, key_row_list = [], []
    for _, k_cols, _, col_places in sets:
        key = line(key_rows * k_cols)
        key_row = key // k_cols
        key_row_list.append(key_row)
        key_col = first_col + col_places(key - key_row * k_cols)
        seen_cols.append(in_window(query_col, key_col, map_cols))
    for index in range(1, 4):
        weight_copy(index, 0).wait()

    def slot_rows(peer):
        return pl.ds(pl.multiple_of(peer * slot, slot), slot)

    def exchange(src, dst, send, recv, peer):
        return pltpu.make_async_remote_copy(
            src_ref=src.at[slot_rows(peer)],
            dst_ref=dst.at[slot_rows(me)],
            send_sem=send.at[peer],
            recv_sem=recv.at[me],
            device_id=(peer // col_count, peer % col_count),
            device_id_type=pl.DeviceIdType.MESH,
        )

    def send_slots(src, dst, send, recv, first, count):
        def one(p, carry):
            peer = first + (me + p) % count

            @pl.when(peer != me)
            def _():
                exchange(src, dst, send, recv, peer).start()

            @pl.when(peer == me)
            def _():
                dst[slot_rows(me), :] = src[slot_rows(me), :]

            return carry

        lax.fori_loop(0, count, one, 0)

    def wait_slots(src, dst, send, recv, sent):
        def one(peer, carry):
            @pl.when(peer != me)
            def _():
                if sent:
                    exchange(src, dst, send, recv, peer).wait_send()
                else:
                    pltpu.make_async_remote_copy(
                        src_ref=src.at[slot_rows(peer)],
                        dst_ref=dst.at[slot_rows(peer)],
                        send_sem=send.at[peer],
                        recv_sem=recv.at[peer],
                        device_id=(peer // col_count, peer % col_count),
                        device_id_type=pl.DeviceIdType.MESH,
                    ).wait_recv()

            return carry

        lax.fori_loop(0, peers, one, 0)

    halves = DILATION // QUERY_ROWS
    half_peers = peers // halves
    half_slots = half_peers * slot

    def half(turn, carry):
        h = (turn + my_col) % halves

        def step(k, inner):
            block = h + halves * k
            top = first_row + block * QUERY_ROWS
            masks = [
                jnp.where(
                    col_seen & in_window(top + query_row, top + key_row - HALO, map_rows), 0.0, MASKED
                )
                for col_seen, key_row in zip(seen_cols, key_row_list)
            ]
            mask = jnp.concatenate(masks, axis=1).astype(jnp.float32)
            q_rows = pl.ds(pl.multiple_of(block * n_query, n_query), n_query)
            to_rows = pl.ds(pl.multiple_of(k * n_query, n_query), n_query)
            k_rows = []
            for base, k_cols, _, _ in sets:
                stride = QUERY_ROWS * k_cols
                k_rows.append(pl.ds(pl.multiple_of(base + block * stride, 16), key_rows * k_cols))
            for g in range(width // lanes):
                cols = slice(g * lanes, (g + 1) * lanes)
                v_cols = slice(width + g * lanes, width + (g + 1) * lanes)
                att_ref[to_rows, cols] = attend(
                    q_ref[q_rows, cols],
                    jnp.concatenate([kv_ref[rows, cols] for rows in k_rows], axis=0),
                    jnp.concatenate([kv_ref[rows, v_cols] for rows in k_rows], axis=0),
                    full_ref[g * per : (g + 1) * per],
                    mask,
                    head_size,
                )
            return inner

        lax.fori_loop(0, block_rows, step, 0)
        blocks = [h + halves * k for k in range(block_rows)]
        stream = jnp.concatenate(
            [x_ref[pl.ds(pl.multiple_of(at * n_query, n_query), n_query), :] for at in blocks], axis=0
        )
        result = finish(
            att_ref[...], stream, gains_ref[1:2, :], proj_all.at[0], up_all.at[0], down_all.at[0]
        )
        here = line(block_rows * n_query)
        which = here // n_query
        token = (h + halves * which) * n_query + here - which * n_query
        hot = one_hot(h * half_slots + column(half_slots), slot_places(token, places[:7]))
        rows = pl.ds(pl.multiple_of(h * half_slots, half_slots), half_slots)
        send_ref[rows, :] = dot(hot, result).astype(jnp.bfloat16)
        send_slots(send_ref, arrive_ref, go_send, go_recv, h * half_peers, half_peers)
        return carry

    lax.fori_loop(0, halves, half, 0)

    size = group_rows * group_cols
    n_two = pack * size
    query, key = column(n_two), line(n_two)
    query_row, key_row = query // group_cols, key // group_cols
    query_col, key_col = query - query_row * group_cols, key - key_row * group_cols
    query_group, key_group = query // size, key // size
    seen = (
        (query_group == key_group)
        & in_window(query_row - query_group * group_rows, key_row - key_group * group_rows, group_rows)
        & in_window(query_col, key_col, group_cols)
    )
    fill_bias(
        rel_ref.at[:, :, 1], bias_two_ref, full_two_ref, group_rows, group_rows, 0, group_cols,
        lambda col: col, 0, pack,
    )
    for n in range(heads):
        full_two_ref[n] = jnp.where(seen, full_two_ref[n], MASKED)
    for index in range(4):
        weight_copy(index, 1).wait()
    arrivals = peers * slot
    hot = one_hot(column(tokens), group_places(line(arrivals), places))
    wait_slots(send_ref, arrive_ref, go_send, go_recv, False)

    x_two_ref[...] = dot(hot, arrive_ref[...]).astype(jnp.bfloat16)
    gain = gains_ref[2:3, :]
    project(x_two_ref, gain, qkv_all[1, :, :width], q_ref, scale, ((0, tokens),))
    project(x_two_ref, gain, qkv_all[1, :, width:], kv_ref, None, ((0, tokens),))

    def step_two(block, carry):
        rows = pl.ds(pl.multiple_of(block * n_two, n_two), n_two)
        for g in range(width // lanes):
            cols = slice(g * lanes, (g + 1) * lanes)
            v_cols = slice(width + g * lanes, width + (g + 1) * lanes)
            att_two_ref[rows, cols] = attend(
                q_ref[rows, cols],
                kv_ref[rows, cols],
                kv_ref[rows, v_cols],
                full_two_ref[g * per : (g + 1) * per],
                None,
                head_size,
            )
        return carry

    lax.fori_loop(0, tokens // n_two, step_two, 0)

    def half_two(turn, carry):
        h = (turn + my_col) % halves
        rows = pl.ds(pl.multiple_of(h * half_slots, half_slots), half_slots)
        spots = group_places(h * half_slots + column(half_slots), places)
        attended = dot(one_hot(spots, line(tokens)), att_two_ref[...]).astype(jnp.bfloat16)
        reply_ref[rows, :] = finish(
            attended, arrive_ref[rows, :], gains_ref[3:4, :], proj_all.at[1], up_all.at[1], down_all.at[1]
        )
        send_slots(reply_ref, back_ref, back_send, back_recv, h * half_peers, half_peers)
        return carry

    lax.fori_loop(0, halves, half_two, 0)
    wait_slots(send_ref, arrive_ref, go_send, go_recv, True)
    for k in range(len(moves)):

        @pl.when(exists(moves[k][0], moves[k][1]))
        def _(k=k):
            halo_copy(k).wait_send()

    hot = one_hot(slot_places(column(tokens), places[:7]), line(arrivals))
    wait_slots(reply_ref, back_ref, back_send, back_recv, False)
    out_ref[...] = dot(hot, back_ref[...]).astype(jnp.bfloat16)
    wait_slots(reply_ref, back_ref, back_send, back_recv, True)


def body(tokens, norm_gains, qkv_weight, rel_bias, proj_weight, up_weight, down_weight):
    tile_rows, tile_cols, width = tokens.shape
    row_count = lax.axis_size("row")
    col_count = lax.axis_size("col")
    heads = rel_bias.shape[1]
    residue_rows = DILATION // row_count
    residue_cols = DILATION // col_count
    block_rows = tile_rows // DILATION
    block_cols = tile_cols // DILATION
    group_rows = block_rows * row_count
    group_cols = block_cols * col_count
    size = group_rows * group_cols
    pack = max(1, 128 // size)
    peers = row_count * col_count
    count = tile_rows * tile_cols
    slot = -(-(count // peers) // 16) * 16
    places = (
        tile_cols, residue_rows, residue_cols, block_rows, block_cols, col_count, slot, row_count
    )
    geometry = (row_count, col_count, tile_rows, tile_cols, heads, pack, places)
    key_rows = QUERY_ROWS + 2 * HALO
    n_query = QUERY_ROWS * tile_cols
    n_key = key_rows * (tile_cols + 2 * HALO)
    padded = count + 2 * HALO * tile_cols + 2 * HALO * (tile_rows + 2 * HALO)
    chunks = -(-(QUERY_ROWS + key_rows - 1) * tile_cols // 128)
    chunks_two = -(-(2 * group_rows - 1) * group_cols // 128)
    slots = peers * slot
    half = jnp.bfloat16
    weights = (qkv_weight, proj_weight, up_weight, down_weight)
    vmem = pl.BlockSpec(memory_space=pltpu.VMEM)
    hbm = pl.BlockSpec(memory_space=pl.ANY)
    result = pl.pallas_call(
        functools.partial(both_layers, geometry),
        out_shape=jax.ShapeDtypeStruct((count, width), half),
        in_specs=[vmem, vmem, vmem, hbm, hbm, hbm, hbm],
        out_specs=vmem,
        scratch_shapes=[pltpu.VMEM(weight.shape, weight.dtype) for weight in weights]
        + [
            pltpu.VMEM((count, width), half),
            pltpu.VMEM((padded, 2 * width), half),
            pltpu.VMEM((padded, width), half),
            pltpu.VMEM((2 * tile_rows * HALO, width), half),
            pltpu.VMEM((heads, n_query, n_key), jnp.float32),
            pltpu.VMEM((heads, pack * size, pack * size), jnp.float32),
            pltpu.VMEM((chunks, tile_cols * heads, 128), jnp.float32),
            pltpu.VMEM((chunks_two, group_cols * heads, 128), jnp.float32),
            pltpu.VMEM((block_rows * n_query, width), half),
            pltpu.VMEM((count, width), half),
            pltpu.VMEM((slots, width), half),
            pltpu.VMEM((slots, width), half),
            pltpu.VMEM((count, width), half),
            pltpu.VMEM((slots, width), half),
            pltpu.VMEM((slots, width), half),
            pltpu.SemaphoreType.DMA((4, 2)),
            pltpu.SemaphoreType.DMA((8,)),
            pltpu.SemaphoreType.DMA((8,)),
            pltpu.SemaphoreType.DMA((peers,)),
            pltpu.SemaphoreType.DMA((peers,)),
            pltpu.SemaphoreType.DMA((peers,)),
            pltpu.SemaphoreType.DMA((peers,)),
        ],
        compiler_params=pltpu.CompilerParams(
            collective_id=0, has_side_effects=True, vmem_limit_bytes=VMEM_BYTES
        ),
    )(tokens.reshape(count, width), norm_gains, rel_bias.transpose(2, 3, 0, 1), *weights)
    return result.reshape(tile_rows, tile_cols, width)


def solution(mesh):
    placed = (P("row", "col", None), P(), P(), P(), P(), P(), P())
    return jax.shard_map(
        body, mesh=mesh, in_specs=placed, out_specs=P("row", "col", None), check_vma=False
    )
```
